32 devices in a mesh: dp: 4 (over y, x), expert: 8 (over z, core).
Axes of the slice: x: 2, y: 2, z: 4, core: 2. Of those that a mesh axis runs over, the one named last changes fastest.
Arguments:
- latent: bfloat16 [4096, 512], P(('dp', 'expert')), may hold values from -6 to 6
- up_proj: bfloat16 [512, 4096], P(None, 'expert'), may hold values from -0.25 to 0.25
- expert_in: bfloat16 [8, 512, 4096], P('expert'), may hold values from -0.25 to 0.25
- expert_out: bfloat16 [8, 2048, 512], P('expert'), may hold values from -0.125 to 0.125
- routes: int32 [4096, 8], P(('dp', 'expert')), may hold values from 0 to 127, all different within a row; in each aligned block of 128 rows (0 to 127, 128 to 255, ...) at most 13 rows name the same one
- gates: bfloat16 [4096, 8], P(('dp', 'expert')), may hold values from 0.099609375 to 1
- cotangent: bfloat16 [4096, 4096], P('dp', 'expert'), may hold values from -6 to 6
Outputs:
- mixed: bfloat16 [4096, 4096], P('dp', 'expert')
- grad_up: float32 [512, 4096], P(None, 'expert')
The draws below stay inside these ranges and needn't reach their ends.
Inputs may be any that keep to these rules, and one draw needn't show every extreme that they name: `routes`: in each aligned block of 128 rows (the tokens of one device) no expert is named more than 13 times.
All inputs are finite; a program needn't handle non-finite values.
Results may differ from the reference program's by a relative error of at most 0.0064.
Values may be sent and summed in bfloat16 or wider, within the bound.
A program may use at most 64 MiB of HBM per device.

```python
import math
import jax
import jax.numpy as jnp
import numpy as np
from jax import lax

D = 4096
L = 512
H = 2048
EXPERTS = 128
TOP = 8
TOK_DEV = 128
CAP = 13
FLY = 8
TOKENS = 4096


def levels(own_key, extent, shards, smallest, largest):
    def one(position, shards_of):
        heights = jax.random.uniform(jax.random.fold_in(jax.random.fold_in(own_key, 6), position), (shards_of,), jnp.float32, smallest / len(shards), largest / len(shards))
        return jnp.repeat(jnp.exp(heights), extent[position] // shards_of).reshape((-1,) + (1,) * (len(extent) - position - 1))

    gain = one(*shards[0])
    for cut in shards[1:]:
        gain = gain * one(*cut)
    return gain


def routed_block(rng, own, number, rows, count, top, most, slope):
    sequence = jax.random.permutation(rng, count)
    heavy_load, usual = load_shares(count, rows * top, most, slope, True), load_shares(count, rows * top, most, slope, False)
    places = jnp.arange(count)

    def named(tallies, rotation):
        used = int((tallies > 0).sum())
        fixed = max(1, used // 4)
        shifted = fixed + (places - fixed + rotation * (used - fixed)) % max(1, count - fixed)
        return jnp.zeros((count,), jnp.int32).at[sequence[jnp.where(places < fixed, places, shifted)]].set(jnp.asarray(tallies, jnp.int32))

    tallies = jnp.where(number % 4 == 0, named(heavy_load, number // 4), named(usual, number - number // 4 - 1))
    mixed = jax.random.permutation(jax.random.fold_in(own, 3), count)
    giver, sink = mixed[0:count // 2 * 2:2], mixed[1:count // 2 * 2:2]
    room = jnp.minimum(tallies[giver] - 1, most - tallies[sink]) // 2
    room = jnp.where((giver == sequence[0]) | (sink == sequence[0]) | (tallies[sink] == 0), 0, jnp.maximum(room, 0))
    shifted = jax.random.randint(jax.random.fold_in(own, 4), (count // 2,), 0, 1 << 20) % (room + 1)
    tallies = tallies.at[giver].add(-shifted).at[sink].add(shifted)
    members = jnp.searchsorted(jnp.cumsum(tallies), jnp.arange(rows * top), side="right").astype(jnp.int32)
    listing = members.reshape(top, rows).T
    listing = listing[jax.random.permutation(jax.random.fold_in(own, 1), rows)]
    rotation = jax.random.randint(jax.random.fold_in(own, 2), (rows, 1), 0, top)
    return jnp.take_along_axis(listing, (jnp.arange(top)[None, :] + rotation) % top, axis=1)


def load_shares(number_of, total, bound, slope, full):
    portions = [(1 << 20) // math.isqrt(standing ** slope) + 1 for standing in range(1, number_of + 1)]
    largest = bound if full else min(bound, max(-(-total // number_of), total * portions[0] // sum(portions)))
    least = 1 if total - largest >= number_of - 1 else 0
    holding, surplus = [largest] + [least] * (number_of - 1), total - largest - least * (number_of - 1)
    while surplus > 0:
        movable = [i for i in range(1, number_of) if holding[i] < largest] or [i for i in range(1, number_of) if holding[i] < bound]
        pool, budget = sum([portions[i] for i in movable]), surplus
        for i in movable:
            extra = min(bound - holding[i], max(1, budget * portions[i] // pool), surplus)
            holding[i] = holding[i] + extra
            surplus = surplus - extra
    return np.array(holding)


def normal_values(own_key, shape, width, limit, pieces=(), kind=jnp.bfloat16):
    result = width * jax.random.normal(own_key, shape, jnp.float32)
    if pieces:
        result = result * levels(own_key, shape, pieces, -0.22, 0.18)
    return jnp.clip(result, -limit, limit).astype(kind)


def setup_inputs(seed: int = 0) -> dict:
    key_list = jax.random.split(jax.random.key(seed), 8)
    latent = normal_values(key_list[0], (TOKENS, L), 1.0, 6.0, ((0, 32),))
    up_proj = normal_values(key_list[1], (L, D), L ** -0.5, 0.25, ((1, 8),))
    expert_in = normal_values(key_list[2], (FLY, L, 2 * H), L ** -0.5, 0.25, ((0, 8),))
    expert_out = normal_values(key_list[3], (FLY, H, L), H ** -0.5, 0.125, ((0, 8),))
    routes_keys = jax.random.split(jax.random.fold_in(key_list[4], 1), TOKENS // TOK_DEV)
    routes_turns = jax.random.permutation(jax.random.fold_in(key_list[4], 3), TOKENS // TOK_DEV)
    routes = jax.vmap(lambda own, number: routed_block(jax.random.fold_in(key_list[4], 2), own, number, TOK_DEV, EXPERTS, TOP, CAP, 2))(routes_keys, routes_turns).reshape((TOKENS, TOP))
    gates = jnp.clip(jnp.exp(math.log(1.0) - 2.306499 * jax.random.uniform(key_list[5], (TOKENS, TOP), jnp.float32) ** levels(key_list[5], (TOKENS, TOP), ((0, 32),), -0.2, 0.2)), 0.099609375, 1.0).astype(jnp.bfloat16)
    cotangent = normal_values(key_list[6], (TOKENS, D), 1.0, 6.0, ((0, 4), (1, 8)))
    return dict(latent=latent, up_proj=up_proj, expert_in=expert_in, expert_out=expert_out, routes=routes, gates=gates, cotangent=cotangent)


def run_expert(item):
    arrived, weight_in, weight_out = item
    hidden = weight_out.shape[0]
    gated = jnp.dot(arrived, weight_in, preferred_element_type=jnp.float32)
    act = (jax.nn.silu(gated[:, :hidden]) * gated[:, hidden:]).astype(jnp.bfloat16)
    return jnp.dot(act, weight_out, preferred_element_type=jnp.float32).astype(jnp.bfloat16)


def reference(latent, up_proj, expert_in, expert_out, routes, gates, cotangent):
    blocks = TOKENS // TOK_DEV
    flat = routes.reshape(blocks, TOK_DEV * TOP).astype(jnp.int32)
    onehot = (flat[:, :, None] == jnp.arange(FLY, dtype=jnp.int32)[None, None, :]).astype(jnp.int32)
    before = jnp.cumsum(onehot, axis=1).astype(jnp.int32) - onehot
    slot = jnp.sum(before * onehot, axis=2).astype(jnp.int32)
    inside = (flat < FLY).reshape(-1)
    row = (jnp.arange(blocks, dtype=jnp.int32)[:, None] * CAP + slot).reshape(-1).astype(jnp.int32)
    which = jnp.where(inside, flat.reshape(-1), FLY).astype(jnp.int32)
    source = jnp.repeat(latent, TOP, axis=0)
    buffers = jnp.zeros((FLY, blocks * CAP, L), jnp.bfloat16).at[which, row].set(source, mode="drop")
    outputs = lax.map(run_expert, (buffers, expert_in, expert_out))
    picked = outputs[jnp.minimum(which, FLY - 1), row].astype(jnp.float32)
    weight = jnp.where(inside, gates.reshape(-1).astype(jnp.float32), jnp.float32(0.0))
    combined = jnp.sum((picked * weight[:, None]).reshape(TOKENS, TOP, L), axis=1).astype(jnp.bfloat16)
    mixed = jnp.dot(combined, up_proj, preferred_element_type=jnp.float32).astype(jnp.bfloat16)
    grad_up = jnp.dot(combined.T, cotangent, preferred_element_type=jnp.float32)
    return mixed, grad_up
```

```python
import functools

import jax
import jax.numpy as jnp
from jax import lax
from jax.experimental import pallas as pl
from jax.experimental.pallas import tpu as pltpu
from jax.sharding import PartitionSpec as P

MESH = pl.DeviceIdType.MESH
SLOTS = 16
CORES = 2


def each(count, step):
    if count <= 8:
        for i in range(count):
            step(i)
    else:
        lax.fori_loop(0, count, lambda i, carry: (step(i), carry)[1], 0)


def kernel(
    n_e, n_dp, chunks,
    routes_ref, gates_ref, latent_ref, up_hbm, win_hbm, wout_hbm, cot_hbm,
    mixed_hbm, grad_hbm,
    win, wout, cot, up, dsend, drecv, act, rsend, gbuf, weight, comb, mixed, gsend, rsbuf, asend,
    load_sem, d_send, d_recv, g_send, g_recv, f_send, r_send, r_recv, a_send, a_recv, own_sem, out_sem,
):
    me = lax.axis_index("expert")
    dp = lax.axis_index("dp")
    n_z = n_e // CORES
    z, core = me // CORES, lax.rem(me, CORES)
    sibling = z * CORES + (CORES - 1 - core)
    z_peers = [lax.rem(z + off, n_z) * CORES + core for off in range(1, n_z)]
    f_peers = [lax.rem(z + off, n_z) * CORES + (CORES - 1 - core) for off in range(1, n_z)]
    e_peers = [lax.rem(me + off, n_e) for off in range(1, n_e)]
    dp_peers = [lax.rem(dp + off, n_dp) for off in range(1, n_dp)]

    barrier = pltpu.get_barrier_semaphore()
    for peer in e_peers:
        pl.semaphore_signal(barrier, inc=1, device_id={"expert": peer}, device_id_type=MESH)
    for peer in dp_peers:
        pl.semaphore_signal(barrier, inc=1, device_id={"dp": peer}, device_id_type=MESH)

    loads = [
        pltpu.make_async_copy(src, dst, load_sem.at[i])
        for i, (src, dst) in enumerate(
            ((win_hbm.at[0], win), (wout_hbm.at[0], wout), (cot_hbm, cot), (up_hbm, up))
        )
    ]
    for load in loads:
        load.start()

    tok = latent_ref.shape[0]
    width = latent_ref.shape[1]
    hidden = wout.shape[0]
    top = routes_ref.shape[0]
    rows = n_e * SLOTS
    cols = width // chunks
    share = cols // n_dp
    meta_parts = (2 * n_e) // SLOTS

    expert_of = lax.broadcasted_iota(jnp.int32, (n_e, tok), 0)
    named = jnp.zeros((n_e, tok), jnp.float32)
    gate = jnp.zeros((n_e, tok), jnp.float32)
    for k in range(top):
        hit = routes_ref[k : k + 1, :] == expert_of
        named = jnp.where(hit, 1.0, named)
        gate = jnp.where(hit, gates_ref[k : k + 1, :].astype(jnp.float32), gate)
    earlier = lax.broadcasted_iota(jnp.int32, (tok, tok), 0) < lax.broadcasted_iota(
        jnp.int32, (tok, tok), 1
    )
    before = jnp.dot(
        named.astype(jnp.bfloat16),
        jnp.where(earlier, 1.0, 0.0).astype(jnp.bfloat16),
        preferred_element_type=jnp.float32,
    )
    slot = jnp.where(named > 0.0, before, -1.0)
    slot_of = lax.broadcasted_iota(jnp.int32, (SLOTS, tok), 0).astype(jnp.float32)
    pick = jnp.concatenate(
        [jnp.where(slot[e : e + 1, :] == slot_of, 1.0, 0.0) for e in range(n_e)], axis=0
    ).astype(jnp.bfloat16)
    outgoing = jnp.dot(pick, latent_ref[...], preferred_element_type=jnp.float32)
    dsend[:, :, :width] = outgoing.astype(jnp.bfloat16).reshape(n_e, SLOTS, width)
    meta = jnp.concatenate([slot, gate], axis=0).astype(jnp.bfloat16)
    for j in range(meta_parts):
        part = meta[j * SLOTS : (j + 1) * SLOTS, :]
        dsend[:, :, width + j * tok : width + (j + 1) * tok] = jnp.broadcast_to(
            part[None], (n_e, SLOTS, tok)
        )
    drecv[me] = dsend[me]

    pl.semaphore_wait(barrier, n_e - 1 + n_dp - 1)

    def dispatch(slot_, peer):
        return pltpu.make_async_remote_copy(
            src_ref=dsend.at[peer], dst_ref=drecv.at[slot_],
            send_sem=d_send.at[peer], recv_sem=d_recv.at[slot_],
            device_id={"expert": peer}, device_id_type=MESH,
        )

    for peer in e_peers:
        dispatch(me, peer).start()
    loads[0].wait()
    for peer in e_peers:
        dispatch(peer, peer).wait_recv()

    arrived = drecv[:, :, :width].reshape(rows, width)
    tile = min(512, hidden)
    for j in range(hidden // tile):
        g = jnp.dot(arrived, win[:, j * tile : (j + 1) * tile], preferred_element_type=jnp.float32)
        u = jnp.dot(
            arrived, win[:, hidden + j * tile : hidden + (j + 1) * tile],
            preferred_element_type=jnp.float32,
        )
        act[:, j * tile : (j + 1) * tile] = (g / (1.0 + jnp.exp(-g)) * u).astype(jnp.bfloat16)

    def gather(c, source, peer, peer_slot, src, sems):
        return pltpu.make_async_remote_copy(
            src_ref=src, dst_ref=gbuf.at[c, source],
            send_sem=sems.at[c, peer_slot], recv_sem=g_recv.at[c, source],
            device_id={"expert": peer}, device_id_type=MESH,
        )

    loads[1].wait()
    sends = []
    for c in range(chunks):
        result = jnp.dot(
            act[...], wout[:, c * cols : (c + 1) * cols], preferred_element_type=jnp.float32
        ).astype(jnp.bfloat16)
        rsend[c] = result
        for i, peer in enumerate(z_peers + [sibling]):
            copy = gather(c, me, peer, i, rsend.at[c], g_send)
            copy.start()
            sends.append(copy)
        gbuf[c, me] = result

    def weigh(b):
        both = jnp.concatenate(
            [drecv[b, :, width + j * tok : width + (j + 1) * tok] for j in range(meta_parts)], axis=0
        ).astype(jnp.float32)
        spread = jnp.concatenate(
            [
                jnp.where(both[e : e + 1, :] == slot_of, both[n_e + e : n_e + e + 1, :], 0.0)
                for e in range(n_e)
            ],
            axis=0,
        )
        weight[b] = spread.T.astype(jnp.bfloat16)

    each(n_e, weigh)
    loads[2].wait()

    def scatter(c, slot_, peer):
        return pltpu.make_async_remote_copy(
            src_ref=gsend.at[c, peer], dst_ref=rsbuf.at[c, slot_],
            send_sem=r_send.at[c, peer], recv_sem=r_recv.at[c, slot_],
            device_id={"dp": peer}, device_id_type=MESH,
        )

    def spread_sum(c, slot_, peer):
        return pltpu.make_async_remote_copy(
            src_ref=asend.at[c], dst_ref=grad_hbm.at[c, slot_],
            send_sem=a_send.at[c, peer], recv_sem=a_recv.at[c, slot_],
            device_id={"dp": peer}, device_id_type=MESH,
        )

    def own_sum(c):
        return pltpu.make_async_copy(asend.at[c], grad_hbm.at[c, dp], own_sem.at[c])

    def reduce(c):
        total = gsend[c, dp].astype(jnp.float32)
        for peer in dp_peers:
            scatter(c, peer, peer).wait_recv()
            total = total + rsbuf[c, peer].astype(jnp.float32)
        asend[c] = total.astype(jnp.bfloat16)
        for peer in dp_peers:
            spread_sum(c, dp, peer).start()
        own_sum(c).start()

    for c in range(chunks):
        for i, peer in enumerate(z_peers):
            gather(c, peer, peer, i, rsend.at[c], g_send).wait_recv()
            forward = gather(c, peer, sibling, i, gbuf.at[c, peer], f_send)
            forward.start()
            sends.append(forward)
        gather(c, sibling, sibling, n_z - 1, rsend.at[c], g_send).wait_recv()
        for i, peer in enumerate(f_peers):
            gather(c, peer, sibling, i, rsend.at[c], f_send).wait_recv()

        def combine(b):
            at = b * SLOTS
            found = gbuf[c, :, pl.ds(at, SLOTS), :].reshape(rows, cols)
            comb[pl.ds(b * tok, tok), c * cols : (c + 1) * cols] = jnp.dot(
                weight[b], found, preferred_element_type=jnp.float32
            ).astype(jnp.bfloat16)

        each(n_e, combine)
        partial = lax.dot_general(
            comb[:, c * cols : (c + 1) * cols], cot[...], (((0,), (0,)), ((), ())),
            preferred_element_type=jnp.float32,
        )
        gsend[c] = partial.astype(jnp.bfloat16).reshape(n_dp, share, cot.shape[1])
        for peer in dp_peers:
            scatter(c, dp, peer).start()
        if c > 0:
            reduce(c - 1)

    loads[3].wait()

    def project(b):
        at = pl.ds(b * tok, tok)
        mixed[at, :] = jnp.dot(
            comb[at, :], up[...], preferred_element_type=jnp.float32
        ).astype(jnp.bfloat16)

    each(n_e, project)
    out = pltpu.make_async_copy(mixed, mixed_hbm, out_sem)
    out.start()
    reduce(chunks - 1)

    for peer in e_peers:
        dispatch(me, peer).wait_send()
    for copy in sends:
        copy.wait_send()
    for c in range(chunks):
        for peer in dp_peers:
            scatter(c, dp, peer).wait_send()
            spread_sum(c, dp, peer).wait_send()
            spread_sum(c, peer, peer).wait_recv()
        own_sum(c).wait()
    out.wait()


def body(n_e, n_dp, latent, up_proj, expert_in, expert_out, routes, gates, cotangent):
    tok, width = latent.shape
    hidden = expert_out.shape[1]
    group, features = cotangent.shape
    chunks = max(1, min(4, width // (16 * n_dp)))
    cols = width // chunks
    share = cols // n_dp
    rows = n_e * SLOTS
    n_z = n_e // CORES
    wide = width + (2 * n_e // SLOTS) * tok
    vmem = pl.BlockSpec(memory_space=pltpu.VMEM)
    hbm = pl.BlockSpec(memory_space=pl.ANY)
    bf16 = jnp.bfloat16
    dma = pltpu.SemaphoreType.DMA
    mixed, grad = pl.pallas_call(
        functools.partial(kernel, n_e, n_dp, chunks),
        out_shape=(
            jax.ShapeDtypeStruct((group, features), bf16),
            jax.ShapeDtypeStruct((chunks, n_dp, share, features), bf16),
        ),
        in_specs=[vmem, vmem, vmem, hbm, hbm, hbm, hbm],
        out_specs=(hbm, hbm),
        scratch_shapes=[
            pltpu.VMEM((width, 2 * hidden), bf16),
            pltpu.VMEM((hidden, width), bf16),
            pltpu.VMEM((group, features), bf16),
            pltpu.VMEM((width, features), bf16),
            pltpu.VMEM((n_e, SLOTS, wide), bf16),
            pltpu.VMEM((n_e, SLOTS, wide), bf16),
            pltpu.VMEM((rows, hidden), bf16),
            pltpu.VMEM((chunks, rows, cols), bf16),
            pltpu.VMEM((chunks, n_e, rows, cols), bf16),
            pltpu.VMEM((n_e, tok, rows), bf16),
            pltpu.VMEM((group, width), bf16),
            pltpu.VMEM((group, features), bf16),
            pltpu.VMEM((chunks, n_dp, share, features), bf16),
            pltpu.VMEM((chunks, n_dp, share, features), bf16),
            pltpu.VMEM((chunks, share, features), bf16),
            dma((4,)),
            dma((n_e,)),
            dma((n_e,)),
            dma((chunks, n_z)),
            dma((chunks, n_e)),
            dma((chunks, n_z)),
            dma((chunks, n_dp)),
            dma((chunks, n_dp)),
            dma((chunks, n_dp)),
            dma((chunks, n_dp)),
            dma((chunks,)),
            dma,
        ],
        compiler_params=pltpu.CompilerParams(
            collective_id=0, has_side_effects=True, vmem_limit_bytes=56 * 1024 * 1024
        ),
        cost_estimate=pl.CostEstimate(
            flops=2 * rows * width * hidden * 3 + 4 * group * width * features,
            bytes_accessed=6 * hidden * width + 8 * group * features,
            transcendentals=rows * hidden,
        ),
    )(routes.T, gates.T, latent, up_proj, expert_in, expert_out, cotangent)
    return mixed, grad.reshape(width, features).astype(jnp.float32)


def solution(mesh):
    in_specs = (
        P(("dp", "expert"), None),
        P(None, "expert"),
        P("expert", None, None),
        P("expert", None, None),
        P(("dp", "expert"), None),
        P(("dp", "expert"), None),
        P("dp", "expert"),
    )
    out_specs = (P("dp", "expert"), P(None, "expert"))
    return jax.shard_map(
        functools.partial(body, mesh.shape["expert"], mesh.shape["dp"]),
        mesh=mesh, in_specs=in_specs, out_specs=out_specs, check_vma=False,
    )
```

```python
import functools

import jax
import jax.numpy as jnp
from jax import lax
from jax.experimental import pallas as pl
from jax.experimental.pallas import tpu as pltpu
from jax.sharding import PartitionSpec as P

MESH = pl.DeviceIdType.MESH
SLOTS = 16
CORES = 2


def each(count, step):
    if count <= 8:
        for i in range(count):
            step(i)
    else:
        lax.fori_loop(0, count, lambda i, carry: (step(i), carry)[1], 0)


def kernel(
    n_e, n_dp, chunks,
    routes_ref, gates_ref, latent_ref, up_hbm, win_hbm, wout_hbm, cot_hbm,
    mixed_hbm, grad_hbm,
    win, wout, cot, up, dsend, drecv, msend, mrecv, act, rsend, gbuf, weight, comb, mixed, gsend, rsbuf, asend,
    load_sem, d_send, d_recv, m_send, m_recv, g_send, g_recv, r_send, r_recv, a_send, a_recv, own_sem, out_sem,
):
    me = lax.axis_index("expert")
    dp = lax.axis_index("dp")
    n_z = n_e // CORES
    z, core = me // CORES, lax.rem(me, CORES)
    sibling = z * CORES + (CORES - 1 - core)
    z_peers = [lax.rem(z + off, n_z) * CORES + core for off in range(1, n_z)]
    f_peers = [lax.rem(z + off, n_z) * CORES + (CORES - 1 - core) for off in range(1, n_z)]
    e_peers = [lax.rem(me + off, n_e) for off in range(1, n_e)]
    dp_peers = [lax.rem(dp + off, n_dp) for off in range(1, n_dp)]

    barrier = pltpu.get_barrier_semaphore()
    for peer in e_peers:
        pl.semaphore_signal(barrier, inc=1, device_id={"expert": peer}, device_id_type=MESH)
    for peer in dp_peers:
        pl.semaphore_signal(barrier, inc=1, device_id={"dp": peer}, device_id_type=MESH)

    loads = [
        pltpu.make_async_copy(src, dst, load_sem.at[i])
        for i, (src, dst) in enumerate(
            ((win_hbm.at[0], win), (wout_hbm.at[0], wout), (cot_hbm, cot), (up_hbm, up))
        )
    ]
    for load in loads:
        load.start()

    tok = latent_ref.shape[0]
    width = latent_ref.shape[1]
    hidden = wout.shape[0]
    top = routes_ref.shape[0]
    rows = n_e * SLOTS
    cols = width // chunks
    share = cols // n_dp

    expert_of = lax.broadcasted_iota(jnp.int32, (n_e, tok), 0)
    named = jnp.zeros((n_e, tok), jnp.float32)
    gate = jnp.zeros((n_e, tok), jnp.float32)
    for k in range(top):
        hit = routes_ref[k : k + 1, :] == expert_of
        named = jnp.where(hit, 1.0, named)
        gate = jnp.where(hit, gates_ref[k : k + 1, :].astype(jnp.float32), gate)
    earlier = lax.broadcasted_iota(jnp.int32, (tok, tok), 0) < lax.broadcasted_iota(
        jnp.int32, (tok, tok), 1
    )
    before = jnp.dot(
        named.astype(jnp.bfloat16),
        jnp.where(earlier, 1.0, 0.0).astype(jnp.bfloat16),
        preferred_element_type=jnp.float32,
    )
    slot = jnp.where(named > 0.0, before, -1.0)
    slot_of = lax.broadcasted_iota(jnp.int32, (SLOTS, tok), 0).astype(jnp.float32)
    pick = jnp.concatenate(
        [jnp.where(slot[e : e + 1, :] == slot_of, 1.0, 0.0) for e in range(n_e)], axis=0
    ).astype(jnp.bfloat16)
    outgoing = jnp.dot(pick, latent_ref[...], preferred_element_type=jnp.float32)
    dsend[...] = outgoing.astype(jnp.bfloat16).reshape(n_e, SLOTS, width)
    meta = jnp.concatenate([slot, gate], axis=0).astype(jnp.bfloat16)
    msend[...] = meta
    mrecv[me] = meta
    drecv[me] = dsend[me]

    pl.semaphore_wait(barrier, n_e - 1 + n_dp - 1)

    def dispatch(slot_, peer):
        return pltpu.make_async_remote_copy(
            src_ref=dsend.at[peer], dst_ref=drecv.at[slot_],
            send_sem=d_send.at[peer], recv_sem=d_recv.at[slot_],
            device_id={"expert": peer}, device_id_type=MESH,
        )

    def table(slot_, peer):
        return pltpu.make_async_remote_copy(
            src_ref=msend, dst_ref=mrecv.at[slot_],
            send_sem=m_send.at[peer], recv_sem=m_recv.at[slot_],
            device_id={"expert": peer}, device_id_type=MESH,
        )

    for peer in e_peers:
        dispatch(me, peer).start()
    for peer in e_peers:
        table(me, peer).start()
    loads[0].wait()
    for peer in e_peers:
        dispatch(peer, peer).wait_recv()

    arrived = drecv[...].reshape(rows, width)
    tile = min(512, hidden)
    for j in range(hidden // tile):
        g = jnp.dot(arrived, win[:, j * tile : (j + 1) * tile], preferred_element_type=jnp.float32)
        u = jnp.dot(
            arrived, win[:, hidden + j * tile : hidden + (j + 1) * tile],
            preferred_element_type=jnp.float32,
        )
        act[:, j * tile : (j + 1) * tile] = (g / (1.0 + jnp.exp(-g)) * u).astype(jnp.bfloat16)

    def gather(c, source, peer, sem, src):
        return pltpu.make_async_remote_copy(
            src_ref=src, dst_ref=gbuf.at[c, source],
            send_sem=g_send.at[c, sem], recv_sem=g_recv.at[c, source],
            device_id={"expert": peer}, device_id_type=MESH,
        )

    def landed(c, source):
        gather(c, source, sibling, 0, gbuf.at[c, source]).wait_recv()

    sends = []

    def send(c, source, peer, sem, src):
        copy = gather(c, source, peer, sem, src)
        copy.start()
        sends.append(copy)

    relay = n_z == 4
    near = (z + 1 - 2 * lax.rem(z, 2)) * CORES + core
    over = lax.rem(z + 2, n_z) * CORES + core
    far = (n_z - 1 - z) * CORES + core
    direct = [over, near] if relay else z_peers

    loads[1].wait()
    for c in range(chunks):
        result = jnp.dot(
            act[...], wout[:, c * cols : (c + 1) * cols], preferred_element_type=jnp.float32
        ).astype(jnp.bfloat16)
        rsend[c] = result
        for i, peer in enumerate(direct + [sibling]):
            send(c, me, peer, i, rsend.at[c])
        gbuf[c, me] = result

    def first(c):
        sem = len(direct) + 1
        for peer in direct:
            landed(c, peer)
            if relay and peer is over:
                send(c, peer, near, sem, gbuf.at[c, peer])
                sem += 1
            send(c, peer, sibling, sem, gbuf.at[c, peer])
            sem += 1

    def second(c):
        if relay:
            landed(c, far)
            send(c, far, sibling, 2 * n_z - 2, gbuf.at[c, far])
        landed(c, sibling)
        for peer in f_peers:
            landed(c, peer)

    def weigh(b):
        both = mrecv[b].astype(jnp.float32)
        spread = jnp.concatenate(
            [
                jnp.where(both[e : e + 1, :] == slot_of, both[n_e + e : n_e + e + 1, :], 0.0)
                for e in range(n_e)
            ],
            axis=0,
        )
        weight[b] = spread.T.astype(jnp.bfloat16)

    for peer in e_peers:
        table(peer, peer).wait_recv()
    each(n_e, weigh)
    loads[2].wait()

    def scatter(c, slot_, peer):
        return pltpu.make_async_remote_copy(
            src_ref=gsend.at[c, peer], dst_ref=rsbuf.at[c, slot_],
            send_sem=r_send.at[c, peer], recv_sem=r_recv.at[c, slot_],
            device_id={"dp": peer}, device_id_type=MESH,
        )

    def spread_sum(c, slot_, peer):
        return pltpu.make_async_remote_copy(
            src_ref=asend.at[c], dst_ref=grad_hbm.at[c, slot_],
            send_sem=a_send.at[c, peer], recv_sem=a_recv.at[c, slot_],
            device_id={"dp": peer}, device_id_type=MESH,
        )

    def own_sum(c):
        return pltpu.make_async_copy(asend.at[c], grad_hbm.at[c, dp], own_sem.at[c])

    def reduce(c):
        total = gsend[c, dp].astype(jnp.float32)
        for peer in dp_peers:
            scatter(c, peer, peer).wait_recv()
            total = total + rsbuf[c, peer].astype(jnp.float32)
        asend[c] = total.astype(jnp.bfloat16)
        for peer in dp_peers:
            spread_sum(c, dp, peer).start()
        own_sum(c).start()

    first(0)
    for c in range(chunks):
        if c + 1 < chunks:
            first(c + 1)
        second(c)

        def combine(b):
            at = b * SLOTS
            found = gbuf[c, :, pl.ds(at, SLOTS), :].reshape(rows, cols)
            comb[pl.ds(b * tok, tok), c * cols : (c + 1) * cols] = jnp.dot(
                weight[b], found, preferred_element_type=jnp.float32
            ).astype(jnp.bfloat16)

        each(n_e, combine)
        partial = lax.dot_general(
            comb[:, c * cols : (c + 1) * cols], cot[...], (((0,), (0,)), ((), ())),
            preferred_element_type=jnp.float32,
        )
        gsend[c] = partial.astype(jnp.bfloat16).reshape(n_dp, share, cot.shape[1])
        for peer in dp_peers:
            scatter(c, dp, peer).start()
        if c > 0:
            reduce(c - 1)

    loads[3].wait()

    def project(b):
        at = pl.ds(b * tok, tok)
        mixed[at, :] = jnp.dot(
            comb[at, :], up[...], preferred_element_type=jnp.float32
        ).astype(jnp.bfloat16)

    each(n_e, project)
    out = pltpu.make_async_copy(mixed, mixed_hbm, out_sem)
    out.start()
    reduce(chunks - 1)

    for peer in e_peers:
        dispatch(me, peer).wait_send()
        table(me, peer).wait_send()
    for copy in sends:
        copy.wait_send()
    for c in range(chunks):
        for peer in dp_peers:
            scatter(c, dp, peer).wait_send()
            spread_sum(c, dp, peer).wait_send()
            spread_sum(c, peer, peer).wait_recv()
        own_sum(c).wait()
    out.wait()


def finish_kernel(parts, mixed_ref, grad_ref, mixed_out, grad_out, narrow, wide, copy_sem, in_sem, out_sem):
    tall, deep = mixed_ref.shape[0] // parts, grad_ref.shape[0] // parts
    copies, outs = [], []
    ins = [
        pltpu.make_async_copy(grad_ref.at[pl.ds(i * deep, deep)], narrow.at[i], in_sem.at[i])
        for i in range(parts)
    ]
    for load in ins:
        load.start()
    for i in range(parts):
        at = pl.ds(i * tall, tall)
        copies.append(pltpu.make_async_copy(mixed_ref.at[at], mixed_out.at[at], copy_sem.at[i]))
        copies[-1].start()
    for i in range(parts):
        ins[i].wait()
        wide[i] = narrow[i].astype(jnp.float32)
        outs.append(
            pltpu.make_async_copy(wide.at[i], grad_out.at[pl.ds(i * deep, deep)], out_sem.at[i])
        )
        outs[-1].start()
    for copy in copies + outs:
        copy.wait()


def finish(mixed, grad):
    parts = 4
    deep, features = grad.shape[0] // parts, grad.shape[1]
    hbm = pl.BlockSpec(memory_space=pl.ANY)
    dma = pltpu.SemaphoreType.DMA
    return pl.pallas_call(
        functools.partial(finish_kernel, parts),
        out_shape=(
            jax.ShapeDtypeStruct(mixed.shape, mixed.dtype),
            jax.ShapeDtypeStruct(grad.shape, jnp.float32),
        ),
        in_specs=[hbm, hbm],
        out_specs=(hbm, hbm),
        scratch_shapes=[
            pltpu.VMEM((parts, deep, features), jnp.bfloat16),
            pltpu.VMEM((parts, deep, features), jnp.float32),
            dma((parts,)),
            dma((parts,)),
            dma((parts,)),
        ],
        compiler_params=pltpu.CompilerParams(vmem_limit_bytes=56 * 1024 * 1024),
    )(mixed, grad)


def body(n_e, n_dp, latent, up_proj, expert_in, expert_out, routes, gates, cotangent):
    tok, width = latent.shape
    hidden = expert_out.shape[1]
    group, features = cotangent.shape
    chunks = max(1, min(4, width // (16 * n_dp)))
    cols = width // chunks
    share = cols // n_dp
    rows = n_e * SLOTS
    n_z = n_e // CORES
    vmem = pl.BlockSpec(memory_space=pltpu.VMEM)
    hbm = pl.BlockSpec(memory_space=pl.ANY)
    bf16 = jnp.bfloat16
    dma = pltpu.SemaphoreType.DMA
    mixed, grad = pl.pallas_call(
        functools.partial(kernel, n_e, n_dp, chunks),
        out_shape=(
            jax.ShapeDtypeStruct((group, features), bf16),
            jax.ShapeDtypeStruct((chunks, n_dp, share, features), bf16),
        ),
        in_specs=[vmem, vmem, vmem, hbm, hbm, hbm, hbm],
        out_specs=(hbm, hbm),
        scratch_shapes=[
            pltpu.VMEM((width, 2 * hidden), bf16),
            pltpu.VMEM((hidden, width), bf16),
            pltpu.VMEM((group, features), bf16),
            pltpu.VMEM((width, features), bf16),
            pltpu.VMEM((n_e, SLOTS, width), bf16),
            pltpu.VMEM((n_e, SLOTS, width), bf16),
            pltpu.VMEM((2 * n_e, tok), bf16),
            pltpu.VMEM((n_e, 2 * n_e, tok), bf16),
            pltpu.VMEM((rows, hidden), bf16),
            pltpu.VMEM((chunks, rows, cols), bf16),
            pltpu.VMEM((chunks, n_e, rows, cols), bf16),
            pltpu.VMEM((n_e, tok, rows), bf16),
            pltpu.VMEM((group, width), bf16),
            pltpu.VMEM((group, features), bf16),
            pltpu.VMEM((chunks, n_dp, share, features), bf16),
            pltpu.VMEM((chunks, n_dp, share, features), bf16),
            pltpu.VMEM((chunks, share, features), bf16),
            dma((4,)),
            dma((n_e,)),
            dma((n_e,)),
            dma((n_e,)),
            dma((n_e,)),
            dma((chunks, 2 * n_z)),
            dma((chunks, n_e)),
            dma((chunks, n_dp)),
            dma((chunks, n_dp)),
            dma((chunks, n_dp)),
            dma((chunks, n_dp)),
            dma((chunks,)),
            dma,
        ],
        compiler_params=pltpu.CompilerParams(
            collective_id=0, has_side_effects=True, vmem_limit_bytes=56 * 1024 * 1024
        ),
        cost_estimate=pl.CostEstimate(
            flops=2 * rows * width * hidden * 3 + 4 * group * width * features,
            bytes_accessed=6 * hidden * width + 8 * group * features,
            transcendentals=rows * hidden,
        ),
    )(routes.T, gates.T, latent, up_proj, expert_in, expert_out, cotangent)
    return finish(mixed, grad.reshape(width, features))


def solution(mesh):
    in_specs = (
        P(("dp", "expert"), None),
        P(None, "expert"),
        P("expert", None, None),
        P("expert", None, None),
        P(("dp", "expert"), None),
        P(("dp", "expert"), None),
        P("dp", "expert"),
    )
    out_specs = (P("dp", "expert"), P(None, "expert"))
    return jax.shard_map(
        functools.partial(body, mesh.shape["expert"], mesh.shape["dp"]),
        mesh=mesh, in_specs=in_specs, out_specs=out_specs, check_vma=False,
    )
```

```python
import functools

import jax
import jax.numpy as jnp
from jax import lax
from jax.experimental import pallas as pl
from jax.experimental.pallas import tpu as pltpu
from jax.sharding import PartitionSpec as P

MESH = pl.DeviceIdType.MESH
SLOTS = 16
CORES = 2


def each(count, step):
    if count <= 8:
        for i in range(count):
            step(i)
    else:
        lax.fori_loop(0, count, lambda i, carry: (step(i), carry)[1], 0)


def kernel(
    n_e, n_dp, chunks,
    routes_ref, gates_ref, latent_ref, up_hbm, win_hbm, wout_hbm, cot_hbm,
    mixed_hbm, grad_hbm,
    win, wout, cot, up, dsend, drecv, act, rsend, gbuf, weight, comb, mixed, gsend, rsbuf, asend,
    load_sem, d_send, d_recv, g_send, g_recv, f_send, r_send, r_recv, a_send, a_recv, own_sem, out_sem,
):
    me = lax.axis_index("expert")
    dp = lax.axis_index("dp")
    n_z = n_e // CORES
    z, core = me // CORES, lax.rem(me, CORES)
    sibling = z * CORES + (CORES - 1 - core)
    z_peers = [lax.rem(z + off, n_z) * CORES + core for off in range(1, n_z)]
    f_peers = [lax.rem(z + off, n_z) * CORES + (CORES - 1 - core) for off in range(1, n_z)]
    e_peers = [lax.rem(me + off, n_e) for off in range(1, n_e)]
    dp_peers = [lax.rem(dp + off, n_dp) for off in range(1, n_dp)]

    barrier = pltpu.get_barrier_semaphore()
    for peer in e_peers:
        pl.semaphore_signal(barrier, inc=1, device_id={"expert": peer}, device_id_type=MESH)
    for peer in dp_peers:
        pl.semaphore_signal(barrier, inc=1, device_id={"dp": peer}, device_id_type=MESH)

    loads = [
        pltpu.make_async_copy(src, dst, load_sem.at[i])
        for i, (src, dst) in enumerate(
            ((win_hbm.at[0], win), (wout_hbm.at[0], wout), (cot_hbm, cot), (up_hbm, up))
        )
    ]
    for load in loads:
        load.start()

    tok = latent_ref.shape[0]
    width = latent_ref.shape[1]
    hidden = wout.shape[0]
    top = routes_ref.shape[0]
    rows = n_e * SLOTS
    cols = width // chunks
    share = cols // n_dp
    meta_parts = (2 * n_e) // SLOTS

    expert_of = lax.broadcasted_iota(jnp.int32, (n_e, tok), 0)
    named = jnp.zeros((n_e, tok), jnp.float32)
    gate = jnp.zeros((n_e, tok), jnp.float32)
    for k in range(top):
        hit = routes_ref[k : k + 1, :] == expert_of
        named = jnp.where(hit, 1.0, named)
        gate = jnp.where(hit, gates_ref[k : k + 1, :].astype(jnp.float32), gate)
    earlier = lax.broadcasted_iota(jnp.int32, (tok, tok), 0) < lax.broadcasted_iota(
        jnp.int32, (tok, tok), 1
    )
    before = jnp.dot(
        named.astype(jnp.bfloat16),
        jnp.where(earlier, 1.0, 0.0).astype(jnp.bfloat16),
        preferred_element_type=jnp.float32,
    )
    slot = jnp.where(named > 0.0, before, -1.0)
    slot_of = lax.broadcasted_iota(jnp.int32, (SLOTS, tok), 0).astype(jnp.float32)
    pick = jnp.concatenate(
        [jnp.where(slot[e : e + 1, :] == slot_of, 1.0, 0.0) for e in range(n_e)], axis=0
    ).astype(jnp.bfloat16)
    outgoing = jnp.dot(pick, latent_ref[...], preferred_element_type=jnp.float32)
    dsend[:, :, :width] = outgoing.astype(jnp.bfloat16).reshape(n_e, SLOTS, width)
    meta = jnp.concatenate([slot, gate], axis=0).astype(jnp.bfloat16)
    for j in range(meta_parts):
        part = meta[j * SLOTS : (j + 1) * SLOTS, :]
        dsend[:, :, width + j * tok : width + (j + 1) * tok] = jnp.broadcast_to(
            part[None], (n_e, SLOTS, tok)
        )
    drecv[me] = dsend[me]

    pl.semaphore_wait(barrier, n_e - 1 + n_dp - 1)

    def dispatch(slot_, peer):
        return pltpu.make_async_remote_copy(
            src_ref=dsend.at[peer], dst_ref=drecv.at[slot_],
            send_sem=d_send.at[peer], recv_sem=d_recv.at[slot_],
            device_id={"expert": peer}, device_id_type=MESH,
        )

    for peer in e_peers:
        dispatch(me, peer).start()
    loads[0].wait()
    for peer in e_peers:
        dispatch(peer, peer).wait_recv()

    arrived = drecv[:, :, :width].reshape(rows, width)
    tile = min(512, hidden)
    for j in range(hidden // tile):
        g = jnp.dot(arrived, win[:, j * tile : (j + 1) * tile], preferred_element_type=jnp.float32)
        u = jnp.dot(
            arrived, win[:, hidden + j * tile : hidden + (j + 1) * tile],
            preferred_element_type=jnp.float32,
        )
        act[:, j * tile : (j + 1) * tile] = (g / (1.0 + jnp.exp(-g)) * u).astype(jnp.bfloat16)

    def gather(c, source, peer, peer_slot, src, sems):
        return pltpu.make_async_remote_copy(
            src_ref=src, dst_ref=gbuf.at[c, source],
            send_sem=sems.at[c, peer_slot], recv_sem=g_recv.at[c, source],
            device_id={"expert": peer}, device_id_type=MESH,
        )

    loads[1].wait()
    sends = []
    for c in range(chunks):
        result = jnp.dot(
            act[...], wout[:, c * cols : (c + 1) * cols], preferred_element_type=jnp.float32
        ).astype(jnp.bfloat16)
        rsend[c] = result
        for i, peer in enumerate(z_peers + [sibling]):
            copy = gather(c, me, peer, i, rsend.at[c], g_send)
            copy.start()
            sends.append(copy)
        gbuf[c, me] = result

    def weigh(b):
        both = jnp.concatenate(
            [drecv[b, :, width + j * tok : width + (j + 1) * tok] for j in range(meta_parts)], axis=0
        ).astype(jnp.float32)
        spread = jnp.concatenate(
            [
                jnp.where(both[e : e + 1, :] == slot_of, both[n_e + e : n_e + e + 1, :], 0.0)
                for e in range(n_e)
            ],
            axis=0,
        )
        weight[b] = spread.T.astype(jnp.bfloat16)

    each(n_e, weigh)
    loads[2].wait()

    def scatter(c, slot_, peer):
        return pltpu.make_async_remote_copy(
            src_ref=gsend.at[c, peer], dst_ref=rsbuf.at[c, slot_],
            send_sem=r_send.at[c, peer], recv_sem=r_recv.at[c, slot_],
            device_id={"dp": peer}, device_id_type=MESH,
        )

    def spread_sum(c, slot_, peer):
        return pltpu.make_async_remote_copy(
            src_ref=asend.at[c], dst_ref=grad_hbm.at[c, slot_],
            send_sem=a_send.at[c, peer], recv_sem=a_recv.at[c, slot_],
            device_id={"dp": peer}, device_id_type=MESH,
        )

    def own_sum(c):
        return pltpu.make_async_copy(asend.at[c], grad_hbm.at[c, dp], own_sem.at[c])

    def reduce(c):
        total = gsend[c, dp].astype(jnp.float32)
        for peer in dp_peers:
            scatter(c, peer, peer).wait_recv()
            total = total + rsbuf[c, peer].astype(jnp.float32)
        asend[c] = total.astype(jnp.bfloat16)
        for peer in dp_peers:
            spread_sum(c, dp, peer).start()
        own_sum(c).start()

    for c in range(chunks):
        for i, peer in enumerate(z_peers):
            gather(c, peer, peer, i, rsend.at[c], g_send).wait_recv()
            forward = gather(c, peer, sibling, i, gbuf.at[c, peer], f_send)
            forward.start()
            sends.append(forward)
        gather(c, sibling, sibling, n_z - 1, rsend.at[c], g_send).wait_recv()
        for i, peer in enumerate(f_peers):
            gather(c, peer, sibling, i, rsend.at[c], f_send).wait_recv()

        def combine(b):
            at = b * SLOTS
            found = gbuf[c, :, pl.ds(at, SLOTS), :].reshape(rows, cols)
            comb[pl.ds(b * tok, tok), c * cols : (c + 1) * cols] = jnp.dot(
                weight[b], found, preferred_element_type=jnp.float32
            ).astype(jnp.bfloat16)

        each(n_e, combine)
        partial = lax.dot_general(
            comb[:, c * cols : (c + 1) * cols], cot[...], (((0,), (0,)), ((), ())),
            preferred_element_type=jnp.float32,
        )
        gsend[c] = partial.astype(jnp.bfloat16).reshape(n_dp, share, cot.shape[1])
        for peer in dp_peers:
            scatter(c, dp, peer).start()
        if c > 0:
            reduce(c - 1)

    loads[3].wait()

    def project(b):
        at = pl.ds(b * tok, tok)
        mixed[at, :] = jnp.dot(
            comb[at, :], up[...], preferred_element_type=jnp.float32
        ).astype(jnp.bfloat16)

    each(n_e, project)
    out = pltpu.make_async_copy(mixed, mixed_hbm, out_sem)
    out.start()
    reduce(chunks - 1)

    for peer in e_peers:
        dispatch(me, peer).wait_send()
    for copy in sends:
        copy.wait_send()
    for c in range(chunks):
        for peer in dp_peers:
            scatter(c, dp, peer).wait_send()
            spread_sum(c, dp, peer).wait_send()
            spread_sum(c, peer, peer).wait_recv()
        own_sum(c).wait()
    out.wait()


def finish_kernel(parts, mixed_ref, grad_ref, mixed_out, grad_out, held, narrow, wide, in_sem, out_sem):
    tall, deep = mixed_ref.shape[0] // parts, grad_ref.shape[0] // parts
    ins, outs = [], []
    for i in range(parts):
        low = pltpu.make_async_copy(
            grad_ref.at[pl.ds(i * deep, deep)], narrow.at[i], in_sem.at[0, i]
        )
        low.start()
        row = pltpu.make_async_copy(
            mixed_ref.at[pl.ds(i * tall, tall)], held.at[i], in_sem.at[1, i]
        )
        row.start()
        ins.append((low, row))
    for i in range(parts):
        low, row = ins[i]
        low.wait()
        wide[i] = narrow[i].astype(jnp.float32)
        outs.append(
            pltpu.make_async_copy(
                wide.at[i], grad_out.at[pl.ds(i * deep, deep)], out_sem.at[0, i]
            )
        )
        outs[-1].start()
        row.wait()
        outs.append(
            pltpu.make_async_copy(
                held.at[i], mixed_out.at[pl.ds(i * tall, tall)], out_sem.at[1, i]
            )
        )
        outs[-1].start()
    for copy in outs:
        copy.wait()


def finish(mixed, grad):
    parts = 4
    deep, features = grad.shape[0] // parts, grad.shape[1]
    hbm = pl.BlockSpec(memory_space=pl.ANY)
    dma = pltpu.SemaphoreType.DMA
    return pl.pallas_call(
        functools.partial(finish_kernel, parts),
        out_shape=(
            jax.ShapeDtypeStruct(mixed.shape, mixed.dtype),
            jax.ShapeDtypeStruct(grad.shape, jnp.float32),
        ),
        in_specs=[hbm, hbm],
        out_specs=(hbm, hbm),
        scratch_shapes=[
            pltpu.VMEM((parts, mixed.shape[0] // parts, features), jnp.bfloat16),
            pltpu.VMEM((parts, deep, features), jnp.bfloat16),
            pltpu.VMEM((parts, deep, features), jnp.float32),
            dma((2, parts)),
            dma((2, parts)),
        ],
        compiler_params=pltpu.CompilerParams(vmem_limit_bytes=56 * 1024 * 1024),
    )(mixed, grad)


def body(n_e, n_dp, latent, up_proj, expert_in, expert_out, routes, gates, cotangent):
    tok, width = latent.shape
    hidden = expert_out.shape[1]
    group, features = cotangent.shape
    chunks = max(1, min(2, width // (16 * n_dp)))
    cols = width // chunks
    share = cols // n_dp
    rows = n_e * SLOTS
    n_z = n_e // CORES
    wide = width + (2 * n_e // SLOTS) * tok
    vmem = pl.BlockSpec(memory_space=pltpu.VMEM)
    hbm = pl.BlockSpec(memory_space=pl.ANY)
    bf16 = jnp.bfloat16
    dma = pltpu.SemaphoreType.DMA
    mixed, grad = pl.pallas_call(
        functools.partial(kernel, n_e, n_dp, chunks),
        out_shape=(
            jax.ShapeDtypeStruct((group, features), bf16),
            jax.ShapeDtypeStruct((chunks, n_dp, share, features), bf16),
        ),
        in_specs=[vmem, vmem, vmem, hbm, hbm, hbm, hbm],
        out_specs=(hbm, hbm),
        scratch_shapes=[
            pltpu.VMEM((width, 2 * hidden), bf16),
            pltpu.VMEM((hidden, width), bf16),
            pltpu.VMEM((group, features), bf16),
            pltpu.VMEM((width, features), bf16),
            pltpu.VMEM((n_e, SLOTS, wide), bf16),
            pltpu.VMEM((n_e, SLOTS, wide), bf16),
            pltpu.VMEM((rows, hidden), bf16),
            pltpu.VMEM((chunks, rows, cols), bf16),
            pltpu.VMEM((chunks, n_e, rows, cols), bf16),
            pltpu.VMEM((n_e, tok, rows), bf16),
            pltpu.VMEM((group, width), bf16),
            pltpu.VMEM((group, features), bf16),
            pltpu.VMEM((chunks, n_dp, share, features), bf16),
            pltpu.VMEM((chunks, n_dp, share, features), bf16),
            pltpu.VMEM((chunks, share, features), bf16),
            dma((4,)),
            dma((n_e,)),
            dma((n_e,)),
            dma((chunks, n_z)),
            dma((chunks, n_e)),
            dma((chunks, n_z)),
            dma((chunks, n_dp)),
            dma((chunks, n_dp)),
            dma((chunks, n_dp)),
            dma((chunks, n_dp)),
            dma((chunks,)),
            dma,
        ],
        compiler_params=pltpu.CompilerParams(
            collective_id=0, has_side_effects=True, vmem_limit_bytes=56 * 1024 * 1024
        ),
        cost_estimate=pl.CostEstimate(
            flops=2 * rows * width * hidden * 3 + 4 * group * width * features,
            bytes_accessed=6 * hidden * width + 8 * group * features,
            transcendentals=rows * hidden,
        ),
    )(routes.T, gates.T, latent, up_proj, expert_in, expert_out, cotangent)
    return finish(mixed, grad.reshape(width, features))


def solution(mesh):
    in_specs = (
        P(("dp", "expert"), None),
        P(None, "expert"),
        P("expert", None, None),
        P("expert", None, None),
        P(("dp", "expert"), None),
        P(("dp", "expert"), None),
        P("dp", "expert"),
    )
    out_specs = (P("dp", "expert"), P(None, "expert"))
    return jax.shard_map(
        functools.partial(body, mesh.shape["expert"], mesh.shape["dp"]),
        mesh=mesh, in_specs=in_specs, out_specs=out_specs, check_vma=False,
    )
```

```python
import functools

import jax
import jax.numpy as jnp
from jax import lax
from jax.experimental import pallas as pl
from jax.experimental.pallas import tpu as pltpu
from jax.sharding import PartitionSpec as P

MESH = pl.DeviceIdType.MESH
SLOTS = 16
CORES = 2


def each(count, step):
    if count <= 8:
        for i in range(count):
            step(i)
    else:
        lax.fori_loop(0, count, lambda i, carry: (step(i), carry)[1], 0)


def kernel(
    n_e, n_dp, chunks,
    routes_ref, gates_ref, latent_ref, up_hbm, win_hbm, wout_hbm, cot_hbm,
    mixed_hbm, grad_hbm,
    win, wout, cot, up, dsend, drecv, msend, mrecv, act, rsend, gbuf, weight, comb, mixed, gsend, rsbuf, asend,
    load_sem, d_send, d_recv, m_send, m_recv, g_send, g_recv, r_send, r_recv, a_send, a_recv, own_sem, out_sem,
):
    me = lax.axis_index("expert")
    dp = lax.axis_index("dp")
    n_z = n_e // CORES
    z, core = me // CORES, lax.rem(me, CORES)
    sibling = z * CORES + (CORES - 1 - core)
    z_peers = [lax.rem(z + off, n_z) * CORES + core for off in range(1, n_z)]
    f_peers = [lax.rem(z + off, n_z) * CORES + (CORES - 1 - core) for off in range(1, n_z)]
    e_peers = [lax.rem(me + off, n_e) for off in range(1, n_e)]
    dp_peers = [lax.rem(dp + off, n_dp) for off in range(1, n_dp)]

    barrier = pltpu.get_barrier_semaphore()
    for peer in e_peers:
        pl.semaphore_signal(barrier, inc=1, device_id={"expert": peer}, device_id_type=MESH)
    for peer in dp_peers:
        pl.semaphore_signal(barrier, inc=1, device_id={"dp": peer}, device_id_type=MESH)

    loads = [
        pltpu.make_async_copy(src, dst, load_sem.at[i])
        for i, (src, dst) in enumerate(
            ((win_hbm.at[0], win), (wout_hbm.at[0], wout), (cot_hbm, cot), (up_hbm, up))
        )
    ]
    for load in loads:
        load.start()

    tok = latent_ref.shape[0]
    width = latent_ref.shape[1]
    hidden = wout.shape[0]
    top = routes_ref.shape[0]
    rows = n_e * SLOTS
    cols = width // chunks
    share = cols // n_dp

    expert_of = lax.broadcasted_iota(jnp.int32, (n_e, tok), 0)
    named = jnp.zeros((n_e, tok), jnp.float32)
    gate = jnp.zeros((n_e, tok), jnp.float32)
    for k in range(top):
        hit = routes_ref[k : k + 1, :] == expert_of
        named = jnp.where(hit, 1.0, named)
        gate = jnp.where(hit, gates_ref[k : k + 1, :].astype(jnp.float32), gate)
    earlier = lax.broadcasted_iota(jnp.int32, (tok, tok), 0) < lax.broadcasted_iota(
        jnp.int32, (tok, tok), 1
    )
    before = jnp.dot(
        named.astype(jnp.bfloat16),
        jnp.where(earlier, 1.0, 0.0).astype(jnp.bfloat16),
        preferred_element_type=jnp.float32,
    )
    slot = jnp.where(named > 0.0, before, -1.0)
    slot_of = lax.broadcasted_iota(jnp.int32, (SLOTS, tok), 0).astype(jnp.float32)
    pick = jnp.concatenate(
        [jnp.where(slot[e : e + 1, :] == slot_of, 1.0, 0.0) for e in range(n_e)], axis=0
    ).astype(jnp.bfloat16)
    outgoing = jnp.dot(pick, latent_ref[...], preferred_element_type=jnp.float32)
    dsend[...] = outgoing.astype(jnp.bfloat16).reshape(n_e, SLOTS, width)
    meta = jnp.concatenate([slot, gate], axis=0).astype(jnp.bfloat16)
    msend[...] = meta
    mrecv[me] = meta
    drecv[me] = dsend[me]

    pl.semaphore_wait(barrier, n_e - 1 + n_dp - 1)

    def dispatch(slot_, peer):
        return pltpu.make_async_remote_copy(
            src_ref=dsend.at[peer], dst_ref=drecv.at[slot_],
            send_sem=d_send.at[peer], recv_sem=d_recv.at[slot_],
            device_id={"expert": peer}, device_id_type=MESH,
        )

    def table(slot_, peer):
        return pltpu.make_async_remote_copy(
            src_ref=msend, dst_ref=mrecv.at[slot_],
            send_sem=m_send.at[peer], recv_sem=m_recv.at[slot_],
            device_id={"expert": peer}, device_id_type=MESH,
        )

    for peer in e_peers:
        dispatch(me, peer).start()
    for peer in e_peers:
        table(me, peer).start()
    loads[0].wait()
    for peer in e_peers:
        dispatch(peer, peer).wait_recv()

    arrived = drecv[...].reshape(rows, width)
    tile = min(512, hidden)
    for j in range(hidden // tile):
        g = jnp.dot(arrived, win[:, j * tile : (j + 1) * tile], preferred_element_type=jnp.float32)
        u = jnp.dot(
            arrived, win[:, hidden + j * tile : hidden + (j + 1) * tile],
            preferred_element_type=jnp.float32,
        )
        act[:, j * tile : (j + 1) * tile] = (g / (1.0 + jnp.exp(-g)) * u).astype(jnp.bfloat16)

    def gather(c, source, peer, sem, src):
        return pltpu.make_async_remote_copy(
            src_ref=src, dst_ref=gbuf.at[c, source],
            send_sem=g_send.at[c, sem], recv_sem=g_recv.at[c, source],
            device_id={"expert": peer}, device_id_type=MESH,
        )

    def landed(c, source):
        gather(c, source, sibling, 0, gbuf.at[c, source]).wait_recv()

    sends = []

    def send(c, source, peer, sem, src):
        copy = gather(c, source, peer, sem, src)
        copy.start()
        sends.append(copy)

    near = (z + 1 - 2 * lax.rem(z, 2)) * CORES + core
    over = lax.rem(z + 2, n_z) * CORES + core
    far = (n_z - 1 - z) * CORES + core
    relayed = [n_z == 4 and 0 < c < chunks - 1 for c in range(chunks)]
    every = [over, far, near] if n_z == 4 else z_peers

    def direct(c):
        return [over, near] if relayed[c] else every

    loads[1].wait()
    for c in range(chunks):
        result = jnp.dot(
            act[...], wout[:, c * cols : (c + 1) * cols], preferred_element_type=jnp.float32
        ).astype(jnp.bfloat16)
        rsend[c] = result
        for i, peer in enumerate(direct(c) + [sibling]):
            send(c, me, peer, i, rsend.at[c])
        gbuf[c, me] = result

    def first(c):
        sem = len(direct(c)) + 1
        for peer in direct(c):
            landed(c, peer)
            if relayed[c] and peer is over:
                send(c, peer, near, sem, gbuf.at[c, peer])
                sem += 1
            send(c, peer, sibling, sem, gbuf.at[c, peer])
            sem += 1

    def second(c):
        if relayed[c]:
            landed(c, far)
            send(c, far, sibling, 2 * n_z - 2, gbuf.at[c, far])
        landed(c, sibling)
        for peer in f_peers:
            landed(c, peer)

    def weigh(b):
        both = mrecv[b].astype(jnp.float32)
        spread = jnp.concatenate(
            [
                jnp.where(both[e : e + 1, :] == slot_of, both[n_e + e : n_e + e + 1, :], 0.0)
                for e in range(n_e)
            ],
            axis=0,
        )
        weight[b] = spread.T.astype(jnp.bfloat16)

    for peer in e_peers:
        table(peer, peer).wait_recv()
    each(n_e, weigh)
    loads[2].wait()

    def scatter(c, slot_, peer):
        return pltpu.make_async_remote_copy(
            src_ref=gsend.at[c, peer], dst_ref=rsbuf.at[c, slot_],
            send_sem=r_send.at[c, peer], recv_sem=r_recv.at[c, slot_],
            device_id={"dp": peer}, device_id_type=MESH,
        )

    def spread_sum(c, slot_, peer):
        return pltpu.make_async_remote_copy(
            src_ref=asend.at[c], dst_ref=grad_hbm.at[c, slot_],
            send_sem=a_send.at[c, peer], recv_sem=a_recv.at[c, slot_],
            device_id={"dp": peer}, device_id_type=MESH,
        )

    def own_sum(c):
        return pltpu.make_async_copy(asend.at[c], grad_hbm.at[c, dp], own_sem.at[c])

    def reduce(c):
        total = gsend[c, dp].astype(jnp.float32)
        for peer in dp_peers:
            scatter(c, peer, peer).wait_recv()
            total = total + rsbuf[c, peer].astype(jnp.float32)
        asend[c] = total.astype(jnp.bfloat16)
        for peer in dp_peers:
            spread_sum(c, dp, peer).start()
        own_sum(c).start()

    for c in range(chunks):
        if not relayed[c]:
            first(c)
        elif not relayed[c - 1]:
            for later in range(c, chunks - 1):
                first(later)
        second(c)

        def combine(b):
            at = b * SLOTS
            found = gbuf[c, :, pl.ds(at, SLOTS), :].reshape(rows, cols)
            comb[pl.ds(b * tok, tok), c * cols : (c + 1) * cols] = jnp.dot(
                weight[b], found, preferred_element_type=jnp.float32
            ).astype(jnp.bfloat16)

        each(n_e, combine)
        partial = lax.dot_general(
            comb[:, c * cols : (c + 1) * cols], cot[...], (((0,), (0,)), ((), ())),
            preferred_element_type=jnp.float32,
        )
        gsend[c] = partial.astype(jnp.bfloat16).reshape(n_dp, share, cot.shape[1])
        for peer in dp_peers:
            scatter(c, dp, peer).start()
        if c > 0:
            reduce(c - 1)

    loads[3].wait()

    def project(b):
        at = pl.ds(b * tok, tok)
        mixed[at, :] = jnp.dot(
            comb[at, :], up[...], preferred_element_type=jnp.float32
        ).astype(jnp.bfloat16)

    each(n_e, project)
    out = pltpu.make_async_copy(mixed, mixed_hbm, out_sem)
    out.start()
    reduce(chunks - 1)

    for peer in e_peers:
        dispatch(me, peer).wait_send()
        table(me, peer).wait_send()
    for copy in sends:
        copy.wait_send()
    for c in range(chunks):
        for peer in dp_peers:
            scatter(c, dp, peer).wait_send()
            spread_sum(c, dp, peer).wait_send()
            spread_sum(c, peer, peer).wait_recv()
        own_sum(c).wait()
    out.wait()


def finish_kernel(parts, mixed_ref, grad_ref, mixed_out, grad_out, held, narrow, wide, in_sem, out_sem):
    tall, deep = mixed_ref.shape[0] // parts, grad_ref.shape[0] // parts
    ins, outs = [], []
    for i in range(parts):
        low = pltpu.make_async_copy(
            grad_ref.at[pl.ds(i * deep, deep)], narrow.at[i], in_sem.at[0, i]
        )
        low.start()
        row = pltpu.make_async_copy(
            mixed_ref.at[pl.ds(i * tall, tall)], held.at[i], in_sem.at[1, i]
        )
        row.start()
        ins.append((low, row))
    for i in range(parts):
        low, row = ins[i]
        low.wait()
        wide[i] = narrow[i].astype(jnp.float32)
        outs.append(
            pltpu.make_async_copy(
                wide.at[i], grad_out.at[pl.ds(i * deep, deep)], out_sem.at[0, i]
            )
        )
        outs[-1].start()
        row.wait()
        outs.append(
            pltpu.make_async_copy(
                held.at[i], mixed_out.at[pl.ds(i * tall, tall)], out_sem.at[1, i]
            )
        )
        outs[-1].start()
    for copy in outs:
        copy.wait()


def finish(mixed, grad):
    parts = 4
    deep, features = grad.shape[0] // parts, grad.shape[1]
    hbm = pl.BlockSpec(memory_space=pl.ANY)
    dma = pltpu.SemaphoreType.DMA
    return pl.pallas_call(
        functools.partial(finish_kernel, parts),
        out_shape=(
            jax.ShapeDtypeStruct(mixed.shape, mixed.dtype),
            jax.ShapeDtypeStruct(grad.shape, jnp.float32),
        ),
        in_specs=[hbm, hbm],
        out_specs=(hbm, hbm),
        scratch_shapes=[
            pltpu.VMEM((parts, mixed.shape[0] // parts, features), jnp.bfloat16),
            pltpu.VMEM((parts, deep, features), jnp.bfloat16),
            pltpu.VMEM((parts, deep, features), jnp.float32),
            dma((2, parts)),
            dma((2, parts)),
        ],
        compiler_params=pltpu.CompilerParams(vmem_limit_bytes=56 * 1024 * 1024),
    )(mixed, grad)


def body(n_e, n_dp, latent, up_proj, expert_in, expert_out, routes, gates, cotangent):
    tok, width = latent.shape
    hidden = expert_out.shape[1]
    group, features = cotangent.shape
    chunks = max(1, min(4, width // (16 * n_dp)))
    cols = width // chunks
    share = cols // n_dp
    rows = n_e * SLOTS
    n_z = n_e // CORES
    vmem = pl.BlockSpec(memory_space=pltpu.VMEM)
    hbm = pl.BlockSpec(memory_space=pl.ANY)
    bf16 = jnp.bfloat16
    dma = pltpu.SemaphoreType.DMA
    mixed, grad = pl.pallas_call(
        functools.partial(kernel, n_e, n_dp, chunks),
        out_shape=(
            jax.ShapeDtypeStruct((group, features), bf16),
            jax.ShapeDtypeStruct((chunks, n_dp, share, features), bf16),
        ),
        in_specs=[vmem, vmem, vmem, hbm, hbm, hbm, hbm],
        out_specs=(hbm, hbm),
        scratch_shapes=[
            pltpu.VMEM((width, 2 * hidden), bf16),
            pltpu.VMEM((hidden, width), bf16),
            pltpu.VMEM((group, features), bf16),
            pltpu.VMEM((width, features), bf16),
            pltpu.VMEM((n_e, SLOTS, width), bf16),
            pltpu.VMEM((n_e, SLOTS, width), bf16),
            pltpu.VMEM((2 * n_e, tok), bf16),
            pltpu.VMEM((n_e, 2 * n_e, tok), bf16),
            pltpu.VMEM((rows, hidden), bf16),
            pltpu.VMEM((chunks, rows, cols), bf16),
            pltpu.VMEM((chunks, n_e, rows, cols), bf16),
            pltpu.VMEM((n_e, tok, rows), bf16),
            pltpu.VMEM((group, width), bf16),
            pltpu.VMEM((group, features), bf16),
            pltpu.VMEM((chunks, n_dp, share, features), bf16),
            pltpu.VMEM((chunks, n_dp, share, features), bf16),
            pltpu.VMEM((chunks, share, features), bf16),
            dma((4,)),
            dma((n_e,)),
            dma((n_e,)),
            dma((n_e,)),
            dma((n_e,)),
            dma((chunks, 2 * n_z)),
            dma((chunks, n_e)),
            dma((chunks, n_dp)),
            dma((chunks, n_dp)),
            dma((chunks, n_dp)),
            dma((chunks, n_dp)),
            dma((chunks,)),
            dma,
        ],
        compiler_params=pltpu.CompilerParams(
            collective_id=0, has_side_effects=True, vmem_limit_bytes=56 * 1024 * 1024
        ),
        cost_estimate=pl.CostEstimate(
            flops=2 * rows * width * hidden * 3 + 4 * group * width * features,
            bytes_accessed=6 * hidden * width + 8 * group * features,
            transcendentals=rows * hidden,
        ),
    )(routes.T, gates.T, latent, up_proj, expert_in, expert_out, cotangent)
    return finish(mixed, grad.reshape(width, features))


def solution(mesh):
    in_specs = (
        P(("dp", "expert"), None),
        P(None, "expert"),
        P("expert", None, None),
        P("expert", None, None),
        P(("dp", "expert"), None),
        P(("dp", "expert"), None),
        P("dp", "expert"),
    )
    out_specs = (P("dp", "expert"), P(None, "expert"))
    return jax.shard_map(
        functools.partial(body, mesh.shape["expert"], mesh.shape["dp"]),
        mesh=mesh, in_specs=in_specs, out_specs=out_specs, check_vma=False,
    )
```

```python
import functools

import jax
import jax.numpy as jnp
from jax import lax
from jax.experimental import pallas as pl
from jax.experimental.pallas import tpu as pltpu
from jax.sharding import PartitionSpec as P

MESH = pl.DeviceIdType.MESH
SLOTS = 16
CAP = 13
CORES = 2


def message_rows(n_e, tok, width):
    return -(-(CAP + n_e * tok // width) // SLOTS) * SLOTS


def each(count, step):
    if count <= 8:
        for i in range(count):
            step(i)
    else:
        lax.fori_loop(0, count, lambda i, carry: (step(i), carry)[1], 0)


def kernel(
    n_e, n_dp, chunks,
    routes_ref, gates_ref, latent_ref, up_hbm, win_hbm, wout_hbm, cot_hbm,
    mixed_hbm, grad_hbm,
    win, wout, cot, up, dsend, drecv, act, rsend, gbuf, weight, comb, mixed, gsend, rsbuf, asend,
    load_sem, d_send, d_recv, g_send, g_recv, f_send, r_send, r_recv, a_send, a_recv, own_sem, out_sem,
):
    me = lax.axis_index("expert")
    dp = lax.axis_index("dp")
    n_z = n_e // CORES
    z, core = me // CORES, lax.rem(me, CORES)
    sibling = z * CORES + (CORES - 1 - core)
    z_peers = [lax.rem(z + off, n_z) * CORES + core for off in range(1, n_z)]
    f_peers = [lax.rem(z + off, n_z) * CORES + (CORES - 1 - core) for off in range(1, n_z)]
    e_peers = [lax.rem(me + off, n_e) for off in range(1, n_e)]
    dp_peers = [lax.rem(dp + off, n_dp) for off in range(1, n_dp)]

    barrier = pltpu.get_barrier_semaphore()
    for peer in e_peers:
        pl.semaphore_signal(barrier, inc=1, device_id={"expert": peer}, device_id_type=MESH)
    for peer in dp_peers:
        pl.semaphore_signal(barrier, inc=1, device_id={"dp": peer}, device_id_type=MESH)

    loads = [
        pltpu.make_async_copy(src, dst, load_sem.at[i])
        for i, (src, dst) in enumerate(
            ((win_hbm.at[0], win), (wout_hbm.at[0], wout), (cot_hbm, cot), (up_hbm, up))
        )
    ]
    for load in loads:
        load.start()

    tok = latent_ref.shape[0]
    width = latent_ref.shape[1]
    hidden = wout.shape[0]
    top = routes_ref.shape[0]
    rows = n_e * SLOTS
    cols = width // chunks
    share = cols // n_dp
    tall = dsend.shape[1]
    per_row = width // tok

    expert_of = lax.broadcasted_iota(jnp.int32, (n_e, tok), 0)
    named = jnp.zeros((n_e, tok), jnp.float32)
    gate = jnp.zeros((n_e, tok), jnp.float32)
    for k in range(top):
        hit = routes_ref[k : k + 1, :] == expert_of
        named = jnp.where(hit, 1.0, named)
        gate = jnp.where(hit, gates_ref[k : k + 1, :].astype(jnp.float32), gate)
    earlier = lax.broadcasted_iota(jnp.int32, (tok, tok), 0) < lax.broadcasted_iota(
        jnp.int32, (tok, tok), 1
    )
    ahead = jnp.where(earlier, 1.0, 0.0).astype(jnp.bfloat16)
    before = jnp.dot(named.astype(jnp.bfloat16), ahead, preferred_element_type=jnp.float32)
    slot = jnp.where(named > 0.0, before, -1.0)
    slot_of = lax.broadcasted_iota(jnp.int32, (SLOTS, tok), 0).astype(jnp.float32)
    pick = jnp.concatenate(
        [jnp.where(slot[e : e + 1, :] == slot_of, 1.0, 0.0) for e in range(n_e)], axis=0
    ).astype(jnp.bfloat16)
    outgoing = jnp.dot(pick, latent_ref[...], preferred_element_type=jnp.float32)
    outgoing = outgoing.reshape(n_e, SLOTS, width)
    if tall > SLOTS:
        outgoing = jnp.concatenate(
            [outgoing, jnp.zeros((n_e, tall - SLOTS, width), jnp.float32)], axis=1
        )
    row_of = lax.broadcasted_iota(jnp.int32, (tall, width), 0)
    extra = jnp.zeros((tall, width), jnp.float32)
    for i in range(n_e // per_row):
        line = jnp.concatenate(
            [gate[e : e + 1, :] for e in range(i * per_row, (i + 1) * per_row)], axis=1
        )
        extra = jnp.where(row_of == CAP + i, line, extra)
    dsend[...] = (outgoing + extra[None]).astype(jnp.bfloat16)
    drecv[me] = dsend[me]

    pl.semaphore_wait(barrier, n_e - 1 + n_dp - 1)

    def dispatch(slot_, peer):
        return pltpu.make_async_remote_copy(
            src_ref=dsend.at[peer], dst_ref=drecv.at[slot_],
            send_sem=d_send.at[peer], recv_sem=d_recv.at[slot_],
            device_id={"expert": peer}, device_id_type=MESH,
        )

    for peer in e_peers:
        dispatch(me, peer).start()
    loads[0].wait()
    for peer in e_peers:
        dispatch(peer, peer).wait_recv()

    arrived = drecv[:, :SLOTS, :].reshape(rows, width)
    tile = min(512, hidden)
    for j in range(hidden // tile):
        g = jnp.dot(arrived, win[:, j * tile : (j + 1) * tile], preferred_element_type=jnp.float32)
        u = jnp.dot(
            arrived, win[:, hidden + j * tile : hidden + (j + 1) * tile],
            preferred_element_type=jnp.float32,
        )
        act[:, j * tile : (j + 1) * tile] = (g / (1.0 + jnp.exp(-g)) * u).astype(jnp.bfloat16)

    def gather(c, source, peer, peer_slot, src, sems):
        return pltpu.make_async_remote_copy(
            src_ref=src, dst_ref=gbuf.at[c, source],
            send_sem=sems.at[c, peer_slot], recv_sem=g_recv.at[c, source],
            device_id={"expert": peer}, device_id_type=MESH,
        )

    loads[1].wait()
    sends = []
    for c in range(chunks):
        result = jnp.dot(
            act[...], wout[:, c * cols : (c + 1) * cols], preferred_element_type=jnp.float32
        ).astype(jnp.bfloat16)
        rsend[c] = result
        for i, peer in enumerate(z_peers + [sibling]):
            copy = gather(c, me, peer, i, rsend.at[c], g_send)
            copy.start()
            sends.append(copy)
        gbuf[c, me] = result

    def weigh(b):
        sent = drecv[b].astype(jnp.float32)
        theirs = jnp.concatenate(
            [
                sent[CAP + e // per_row : CAP + e // per_row + 1, e % per_row * tok : (e % per_row + 1) * tok]
                for e in range(n_e)
            ],
            axis=0,
        )
        live = theirs > 0.0
        count = jnp.dot(
            jnp.where(live, 1.0, 0.0).astype(jnp.bfloat16), ahead, preferred_element_type=jnp.float32
        )
        place = jnp.where(live, count, -1.0)
        spread = jnp.concatenate(
            [
                jnp.where(place[e : e + 1, :] == slot_of, theirs[e : e + 1, :], 0.0)
                for e in range(n_e)
            ],
            axis=0,
        )
        weight[b] = spread.T.astype(jnp.bfloat16)

    each(n_e, weigh)
    loads[2].wait()

    def scatter(c, slot_, peer):
        return pltpu.make_async_remote_copy(
            src_ref=gsend.at[c, peer], dst_ref=rsbuf.at[c, slot_],
            send_sem=r_send.at[c, peer], recv_sem=r_recv.at[c, slot_],
            device_id={"dp": peer}, device_id_type=MESH,
        )

    def spread_sum(c, slot_, peer):
        return pltpu.make_async_remote_copy(
            src_ref=asend.at[c], dst_ref=grad_hbm.at[c, slot_],
            send_sem=a_send.at[c, peer], recv_sem=a_recv.at[c, slot_],
            device_id={"dp": peer}, device_id_type=MESH,
        )

    def own_sum(c):
        return pltpu.make_async_copy(asend.at[c], grad_hbm.at[c, dp], own_sem.at[c])

    def reduce(c):
        total = gsend[c, dp].astype(jnp.float32)
        for peer in dp_peers:
            scatter(c, peer, peer).wait_recv()
            total = total + rsbuf[c, peer].astype(jnp.float32)
        asend[c] = total.astype(jnp.bfloat16)
        for peer in dp_peers:
            spread_sum(c, dp, peer).start()
        own_sum(c).start()

    for c in range(chunks):
        for i, peer in enumerate(z_peers):
            gather(c, peer, peer, i, rsend.at[c], g_send).wait_recv()
            forward = gather(c, peer, sibling, i, gbuf.at[c, peer], f_send)
            forward.start()
            sends.append(forward)
        gather(c, sibling, sibling, n_z - 1, rsend.at[c], g_send).wait_recv()
        for i, peer in enumerate(f_peers):
            gather(c, peer, sibling, i, rsend.at[c], f_send).wait_recv()

        def combine(b):
            at = b * SLOTS
            found = gbuf[c, :, pl.ds(at, SLOTS), :].reshape(rows, cols)
            comb[pl.ds(b * tok, tok), c * cols : (c + 1) * cols] = jnp.dot(
                weight[b], found, preferred_element_type=jnp.float32
            ).astype(jnp.bfloat16)

        each(n_e, combine)
        partial = lax.dot_general(
            comb[:, c * cols : (c + 1) * cols], cot[...], (((0,), (0,)), ((), ())),
            preferred_element_type=jnp.float32,
        )
        gsend[c] = partial.astype(jnp.bfloat16).reshape(n_dp, share, cot.shape[1])
        for peer in dp_peers:
            scatter(c, dp, peer).start()
        if c > 0:
            reduce(c - 1)

    loads[3].wait()

    def project(b):
        at = pl.ds(b * tok, tok)
        mixed[at, :] = jnp.dot(
            comb[at, :], up[...], preferred_element_type=jnp.float32
        ).astype(jnp.bfloat16)

    each(n_e, project)
    out = pltpu.make_async_copy(mixed, mixed_hbm, out_sem)
    out.start()
    reduce(chunks - 1)

    for peer in e_peers:
        dispatch(me, peer).wait_send()
    for copy in sends:
        copy.wait_send()
    for c in range(chunks):
        for peer in dp_peers:
            scatter(c, dp, peer).wait_send()
            spread_sum(c, dp, peer).wait_send()
            spread_sum(c, peer, peer).wait_recv()
        own_sum(c).wait()
    out.wait()


def finish_kernel(parts, mixed_ref, grad_ref, mixed_out, grad_out, held, narrow, wide, in_sem, out_sem):
    tall, deep = mixed_ref.shape[0] // parts, grad_ref.shape[0] // parts
    ins, outs = [], []
    for i in range(parts):
        low = pltpu.make_async_copy(
            grad_ref.at[pl.ds(i * deep, deep)], narrow.at[i], in_sem.at[0, i]
        )
        low.start()
        row = pltpu.make_async_copy(
            mixed_ref.at[pl.ds(i * tall, tall)], held.at[i], in_sem.at[1, i]
        )
        row.start()
        ins.append((low, row))
    for i in range(parts):
        low, row = ins[i]
        low.wait()
        wide[i] = narrow[i].astype(jnp.float32)
        outs.append(
            pltpu.make_async_copy(
                wide.at[i], grad_out.at[pl.ds(i * deep, deep)], out_sem.at[0, i]
            )
        )
        outs[-1].start()
        row.wait()
        outs.append(
            pltpu.make_async_copy(
                held.at[i], mixed_out.at[pl.ds(i * tall, tall)], out_sem.at[1, i]
            )
        )
        outs[-1].start()
    for copy in outs:
        copy.wait()


def finish(mixed, grad):
    parts = 4
    deep, features = grad.shape[0] // parts, grad.shape[1]
    hbm = pl.BlockSpec(memory_space=pl.ANY)
    dma = pltpu.SemaphoreType.DMA
    return pl.pallas_call(
        functools.partial(finish_kernel, parts),
        out_shape=(
            jax.ShapeDtypeStruct(mixed.shape, mixed.dtype),
            jax.ShapeDtypeStruct(grad.shape, jnp.float32),
        ),
        in_specs=[hbm, hbm],
        out_specs=(hbm, hbm),
        scratch_shapes=[
            pltpu.VMEM((parts, mixed.shape[0] // parts, features), jnp.bfloat16),
            pltpu.VMEM((parts, deep, features), jnp.bfloat16),
            pltpu.VMEM((parts, deep, features), jnp.float32),
            dma((2, parts)),
            dma((2, parts)),
        ],
        compiler_params=pltpu.CompilerParams(vmem_limit_bytes=56 * 1024 * 1024),
    )(mixed, grad)


def body(n_e, n_dp, latent, up_proj, expert_in, expert_out, routes, gates, cotangent):
    tok, width = latent.shape
    hidden = expert_out.shape[1]
    group, features = cotangent.shape
    chunks = max(1, min(4, width // (16 * n_dp)))
    cols = width // chunks
    share = cols // n_dp
    rows = n_e * SLOTS
    n_z = n_e // CORES
    tall = message_rows(n_e, tok, width)
    vmem = pl.BlockSpec(memory_space=pltpu.VMEM)
    hbm = pl.BlockSpec(memory_space=pl.ANY)
    bf16 = jnp.bfloat16
    dma = pltpu.SemaphoreType.DMA
    mixed, grad = pl.pallas_call(
        functools.partial(kernel, n_e, n_dp, chunks),
        out_shape=(
            jax.ShapeDtypeStruct((group, features), bf16),
            jax.ShapeDtypeStruct((chunks, n_dp, share, features), bf16),
        ),
        in_specs=[vmem, vmem, vmem, hbm, hbm, hbm, hbm],
        out_specs=(hbm, hbm),
        scratch_shapes=[
            pltpu.VMEM((width, 2 * hidden), bf16),
            pltpu.VMEM((hidden, width), bf16),
            pltpu.VMEM((group, features), bf16),
            pltpu.VMEM((width, features), bf16),
            pltpu.VMEM((n_e, tall, width), bf16),
            pltpu.VMEM((n_e, tall, width), bf16),
            pltpu.VMEM((rows, hidden), bf16),
            pltpu.VMEM((chunks, rows, cols), bf16),
            pltpu.VMEM((chunks, n_e, rows, cols), bf16),
            pltpu.VMEM((n_e, tok, rows), bf16),
            pltpu.VMEM((group, width), bf16),
            pltpu.VMEM((group, features), bf16),
            pltpu.VMEM((chunks, n_dp, share, features), bf16),
            pltpu.VMEM((chunks, n_dp, share, features), bf16),
            pltpu.VMEM((chunks, share, features), bf16),
            dma((4,)),
            dma((n_e,)),
            dma((n_e,)),
            dma((chunks, n_z)),
            dma((chunks, n_e)),
            dma((chunks, n_z)),
            dma((chunks, n_dp)),
            dma((chunks, n_dp)),
            dma((chunks, n_dp)),
            dma((chunks, n_dp)),
            dma((chunks,)),
            dma,
        ],
        compiler_params=pltpu.CompilerParams(
            collective_id=0, has_side_effects=True, vmem_limit_bytes=56 * 1024 * 1024
        ),
        cost_estimate=pl.CostEstimate(
            flops=2 * rows * width * hidden * 3 + 4 * group * width * features,
            bytes_accessed=6 * hidden * width + 8 * group * features,
            transcendentals=rows * hidden,
        ),
    )(routes.T, gates.T, latent, up_proj, expert_in, expert_out, cotangent)
    return finish(mixed, grad.reshape(width, features))


def solution(mesh):
    in_specs = (
        P(("dp", "expert"), None),
        P(None, "expert"),
        P("expert", None, None),
        P("expert", None, None),
        P(("dp", "expert"), None),
        P(("dp", "expert"), None),
        P("dp", "expert"),
    )
    out_specs = (P("dp", "expert"), P(None, "expert"))
    return jax.shard_map(
        functools.partial(body, mesh.shape["expert"], mesh.shape["dp"]),
        mesh=mesh, in_specs=in_specs, out_specs=out_specs, check_vma=False,
    )
```

```python
import functools

import jax
import jax.numpy as jnp
from jax import lax
from jax.experimental import pallas as pl
from jax.experimental.pallas import tpu as pltpu
from jax.sharding import PartitionSpec as P

MESH = pl.DeviceIdType.MESH
SLOTS = 16
CAP = 13
CORES = 2


def message_rows(n_e, tok, width):
    return -(-(CAP + n_e * tok // width) // SLOTS) * SLOTS


def each(count, step):
    if count <= 8:
        for i in range(count):
            step(i)
    else:
        lax.fori_loop(0, count, lambda i, carry: (step(i), carry)[1], 0)


def kernel(
    n_e, n_dp, chunks,
    routes_ref, gates_ref, latent_ref, up_hbm, win_hbm, wout_hbm, cot_hbm,
    mixed, grad,
    win, wout, cot, up, dsend, drecv, act, rsend, gbuf, weight, comb, gsend, rsbuf, asend,
    load_sem, d_send, d_recv, g_send, g_recv, f_send, r_send, r_recv, a_send, a_recv,
):
    me = lax.axis_index("expert")
    dp = lax.axis_index("dp")
    n_z = n_e // CORES
    z, core = me // CORES, lax.rem(me, CORES)
    sibling = z * CORES + (CORES - 1 - core)
    z_peers = [lax.rem(z + off, n_z) * CORES + core for off in range(1, n_z)]
    f_peers = [lax.rem(z + off, n_z) * CORES + (CORES - 1 - core) for off in range(1, n_z)]
    e_peers = [lax.rem(me + off, n_e) for off in range(1, n_e)]
    dp_peers = [lax.rem(dp + off, n_dp) for off in range(1, n_dp)]

    barrier = pltpu.get_barrier_semaphore()
    for peer in e_peers:
        pl.semaphore_signal(barrier, inc=1, device_id={"expert": peer}, device_id_type=MESH)
    for peer in dp_peers:
        pl.semaphore_signal(barrier, inc=1, device_id={"dp": peer}, device_id_type=MESH)

    loads = [
        pltpu.make_async_copy(src, dst, load_sem.at[i])
        for i, (src, dst) in enumerate(
            ((win_hbm.at[0], win), (wout_hbm.at[0], wout), (cot_hbm, cot), (up_hbm, up))
        )
    ]
    for load in loads:
        load.start()

    tok = latent_ref.shape[0]
    width = latent_ref.shape[1]
    hidden = wout.shape[0]
    top = routes_ref.shape[0]
    rows = n_e * SLOTS
    cols = width // chunks
    share = cols // n_dp
    tall = dsend.shape[1]
    per_row = width // tok

    expert_of = lax.broadcasted_iota(jnp.int32, (n_e, tok), 0)
    named = jnp.zeros((n_e, tok), jnp.float32)
    gate = jnp.zeros((n_e, tok), jnp.float32)
    for k in range(top):
        hit = routes_ref[k : k + 1, :] == expert_of
        named = jnp.where(hit, 1.0, named)
        gate = jnp.where(hit, gates_ref[k : k + 1, :].astype(jnp.float32), gate)
    earlier = lax.broadcasted_iota(jnp.int32, (tok, tok), 0) < lax.broadcasted_iota(
        jnp.int32, (tok, tok), 1
    )
    ahead = jnp.where(earlier, 1.0, 0.0).astype(jnp.bfloat16)
    before = jnp.dot(named.astype(jnp.bfloat16), ahead, preferred_element_type=jnp.float32)
    slot = jnp.where(named > 0.0, before, -1.0)
    slot_of = lax.broadcasted_iota(jnp.int32, (SLOTS, tok), 0).astype(jnp.float32)
    pick = jnp.concatenate(
        [jnp.where(slot[e : e + 1, :] == slot_of, 1.0, 0.0) for e in range(n_e)], axis=0
    ).astype(jnp.bfloat16)
    outgoing = jnp.dot(pick, latent_ref[...], preferred_element_type=jnp.float32)
    outgoing = outgoing.reshape(n_e, SLOTS, width)
    if tall > SLOTS:
        outgoing = jnp.concatenate(
            [outgoing, jnp.zeros((n_e, tall - SLOTS, width), jnp.float32)], axis=1
        )
    row_of = lax.broadcasted_iota(jnp.int32, (tall, width), 0)
    extra = jnp.zeros((tall, width), jnp.float32)
    for i in range(n_e // per_row):
        line = jnp.concatenate(
            [gate[e : e + 1, :] for e in range(i * per_row, (i + 1) * per_row)], axis=1
        )
        extra = jnp.where(row_of == CAP + i, line, extra)
    dsend[...] = (outgoing + extra[None]).astype(jnp.bfloat16)
    drecv[me] = dsend[me]

    pl.semaphore_wait(barrier, n_e - 1 + n_dp - 1)

    def dispatch(slot_, peer):
        return pltpu.make_async_remote_copy(
            src_ref=dsend.at[peer], dst_ref=drecv.at[slot_],
            send_sem=d_send.at[peer], recv_sem=d_recv.at[slot_],
            device_id={"expert": peer}, device_id_type=MESH,
        )

    for peer in e_peers:
        dispatch(me, peer).start()
    loads[0].wait()
    for peer in e_peers:
        dispatch(peer, peer).wait_recv()

    arrived = drecv[:, :SLOTS, :].reshape(rows, width)
    tile = min(512, hidden)
    for j in range(hidden // tile):
        g = jnp.dot(arrived, win[:, j * tile : (j + 1) * tile], preferred_element_type=jnp.float32)
        u = jnp.dot(
            arrived, win[:, hidden + j * tile : hidden + (j + 1) * tile],
            preferred_element_type=jnp.float32,
        )
        act[:, j * tile : (j + 1) * tile] = (g / (1.0 + jnp.exp(-g)) * u).astype(jnp.bfloat16)

    def gather(c, source, peer, peer_slot, src, sems):
        return pltpu.make_async_remote_copy(
            src_ref=src, dst_ref=gbuf.at[c, source],
            send_sem=sems.at[c, peer_slot], recv_sem=g_recv.at[c, source],
            device_id={"expert": peer}, device_id_type=MESH,
        )

    loads[1].wait()
    sends = []
    for c in range(chunks):
        result = jnp.dot(
            act[...], wout[:, c * cols : (c + 1) * cols], preferred_element_type=jnp.float32
        ).astype(jnp.bfloat16)
        rsend[c] = result
        for i, peer in enumerate(z_peers + [sibling]):
            copy = gather(c, me, peer, i, rsend.at[c], g_send)
            copy.start()
            sends.append(copy)
        gbuf[c, me] = result

    def weigh(b):
        sent = drecv[b].astype(jnp.float32)
        theirs = jnp.concatenate(
            [
                sent[CAP + e // per_row : CAP + e // per_row + 1, e % per_row * tok : (e % per_row + 1) * tok]
                for e in range(n_e)
            ],
            axis=0,
        )
        live = theirs > 0.0
        count = jnp.dot(
            jnp.where(live, 1.0, 0.0).astype(jnp.bfloat16), ahead, preferred_element_type=jnp.float32
        )
        place = jnp.where(live, count, -1.0)
        spread = jnp.concatenate(
            [
                jnp.where(place[e : e + 1, :] == slot_of, theirs[e : e + 1, :], 0.0)
                for e in range(n_e)
            ],
            axis=0,
        )
        weight[b] = spread.T.astype(jnp.bfloat16)

    each(n_e, weigh)
    loads[2].wait()

    def scatter(c, slot_, peer):
        return pltpu.make_async_remote_copy(
            src_ref=gsend.at[c, peer], dst_ref=rsbuf.at[c, slot_],
            send_sem=r_send.at[c, peer], recv_sem=r_recv.at[c, slot_],
            device_id={"dp": peer}, device_id_type=MESH,
        )

    def spread_sum(c, slot_, peer):
        return pltpu.make_async_remote_copy(
            src_ref=asend.at[c], dst_ref=grad.at[c, slot_],
            send_sem=a_send.at[c, peer], recv_sem=a_recv.at[c, slot_],
            device_id={"dp": peer}, device_id_type=MESH,
        )

    def reduce(c):
        total = gsend[c, dp].astype(jnp.float32)
        for peer in dp_peers:
            scatter(c, peer, peer).wait_recv()
            total = total + rsbuf[c, peer].astype(jnp.float32)
        asend[c] = total.astype(jnp.bfloat16)
        for peer in dp_peers:
            spread_sum(c, dp, peer).start()
        grad[c, dp] = asend[c]

    for c in range(chunks):
        for i, peer in enumerate(z_peers):
            gather(c, peer, peer, i, rsend.at[c], g_send).wait_recv()
            forward = gather(c, peer, sibling, i, gbuf.at[c, peer], f_send)
            forward.start()
            sends.append(forward)
        gather(c, sibling, sibling, n_z - 1, rsend.at[c], g_send).wait_recv()
        for i, peer in enumerate(f_peers):
            gather(c, peer, sibling, i, rsend.at[c], f_send).wait_recv()

        def combine(b):
            at = b * SLOTS
            found = gbuf[c, :, pl.ds(at, SLOTS), :].reshape(rows, cols)
            comb[pl.ds(b * tok, tok), c * cols : (c + 1) * cols] = jnp.dot(
                weight[b], found, preferred_element_type=jnp.float32
            ).astype(jnp.bfloat16)

        each(n_e, combine)
        partial = lax.dot_general(
            comb[:, c * cols : (c + 1) * cols], cot[...], (((0,), (0,)), ((), ())),
            preferred_element_type=jnp.float32,
        )
        gsend[c] = partial.astype(jnp.bfloat16).reshape(n_dp, share, cot.shape[1])
        for peer in dp_peers:
            scatter(c, dp, peer).start()
        if c > 0:
            reduce(c - 1)

    loads[3].wait()

    def project(b):
        at = pl.ds(b * tok, tok)
        mixed[at, :] = jnp.dot(
            comb[at, :], up[...], preferred_element_type=jnp.float32
        ).astype(jnp.bfloat16)

    half = n_e // 2
    each(half, project)
    reduce(chunks - 1)
    each(n_e - half, lambda b: project(half + b))

    for peer in e_peers:
        dispatch(me, peer).wait_send()
    for copy in sends:
        copy.wait_send()
    for c in range(chunks):
        for peer in dp_peers:
            scatter(c, dp, peer).wait_send()
            spread_sum(c, dp, peer).wait_send()
            spread_sum(c, peer, peer).wait_recv()


def finish_kernel(mixed_ref, grad_ref, mixed_out, grad_out, wide, mixed_sem, grad_sem):
    copy = pltpu.make_async_copy(mixed_ref, mixed_out, mixed_sem)
    copy.start()
    chunks, n_dp, share = grad_ref.shape[:3]
    outs = []
    for c in range(chunks):
        wide[c] = grad_ref[c].astype(jnp.float32).reshape(n_dp * share, grad_ref.shape[3])
        at = pl.ds(c * n_dp * share, n_dp * share)
        outs.append(pltpu.make_async_copy(wide.at[c], grad_out.at[at], grad_sem.at[c]))
        outs[-1].start()
    copy.wait()
    for out in outs:
        out.wait()


def finish(mixed, grad):
    chunks, n_dp, share, features = grad.shape
    vmem = pl.BlockSpec(memory_space=pltpu.VMEM)
    hbm = pl.BlockSpec(memory_space=pl.ANY)
    dma = pltpu.SemaphoreType.DMA
    return pl.pallas_call(
        finish_kernel,
        out_shape=(
            jax.ShapeDtypeStruct(mixed.shape, mixed.dtype),
            jax.ShapeDtypeStruct((chunks * n_dp * share, features), jnp.float32),
        ),
        in_specs=[vmem, vmem],
        out_specs=(hbm, hbm),
        scratch_shapes=[
            pltpu.VMEM((chunks, n_dp * share, features), jnp.float32),
            dma,
            dma((chunks,)),
        ],
        compiler_params=pltpu.CompilerParams(vmem_limit_bytes=50 * 1024 * 1024),
    )(mixed, grad)


def body(n_e, n_dp, latent, up_proj, expert_in, expert_out, routes, gates, cotangent):
    tok, width = latent.shape
    hidden = expert_out.shape[1]
    group, features = cotangent.shape
    chunks = max(1, min(4, width // (16 * n_dp)))
    cols = width // chunks
    share = cols // n_dp
    rows = n_e * SLOTS
    n_z = n_e // CORES
    tall = message_rows(n_e, tok, width)
    vmem = pl.BlockSpec(memory_space=pltpu.VMEM)
    hbm = pl.BlockSpec(memory_space=pl.ANY)
    bf16 = jnp.bfloat16
    dma = pltpu.SemaphoreType.DMA
    mixed, grad = pl.pallas_call(
        functools.partial(kernel, n_e, n_dp, chunks),
        out_shape=(
            pltpu.VMEM((group, features), bf16),
            pltpu.VMEM((chunks, n_dp, share, features), bf16),
        ),
        in_specs=[vmem, vmem, vmem, hbm, hbm, hbm, hbm],
        out_specs=(vmem, vmem),
        scratch_shapes=[
            pltpu.VMEM((width, 2 * hidden), bf16),
            pltpu.VMEM((hidden, width), bf16),
            pltpu.VMEM((group, features), bf16),
            pltpu.VMEM((width, features), bf16),
            pltpu.VMEM((n_e, tall, width), bf16),
            pltpu.VMEM((n_e, tall, width), bf16),
            pltpu.VMEM((rows, hidden), bf16),
            pltpu.VMEM((chunks, rows, cols), bf16),
            pltpu.VMEM((chunks, n_e, rows, cols), bf16),
            pltpu.VMEM((n_e, tok, rows), bf16),
            pltpu.VMEM((group, width), bf16),
            pltpu.VMEM((chunks, n_dp, share, features), bf16),
            pltpu.VMEM((chunks, n_dp, share, features), bf16),
            pltpu.VMEM((chunks, share, features), bf16),
            dma((4,)),
            dma((n_e,)),
            dma((n_e,)),
            dma((chunks, n_z)),
            dma((chunks, n_e)),
            dma((chunks, n_z)),
            dma((chunks, n_dp)),
            dma((chunks, n_dp)),
            dma((chunks, n_dp)),
            dma((chunks, n_dp)),
        ],
        compiler_params=pltpu.CompilerParams(
            collective_id=0, has_side_effects=True, vmem_limit_bytes=54 * 1024 * 1024
        ),
        cost_estimate=pl.CostEstimate(
            flops=2 * rows * width * hidden * 3 + 4 * group * width * features,
            bytes_accessed=6 * hidden * width + 8 * group * features,
            transcendentals=rows * hidden,
        ),
    )(routes.T, gates.T, latent, up_proj, expert_in, expert_out, cotangent)
    return finish(mixed, grad)


def solution(mesh):
    in_specs = (
        P(("dp", "expert"), None),
        P(None, "expert"),
        P("expert", None, None),
        P("expert", None, None),
        P(("dp", "expert"), None),
        P(("dp", "expert"), None),
        P("dp", "expert"),
    )
    out_specs = (P("dp", "expert"), P(None, "expert"))
    return jax.shard_map(
        functools.partial(body, mesh.shape["expert"], mesh.shape["dp"]),
        mesh=mesh, in_specs=in_specs, out_specs=out_specs, check_vma=False,
    )
```

```python
import functools

import jax
import jax.numpy as jnp
from jax import lax
from jax.experimental import pallas as pl
from jax.experimental.pallas import tpu as pltpu
from jax.sharding import PartitionSpec as P

MESH = pl.DeviceIdType.MESH
SLOTS = 16
CAP = 13
CORES = 2


def message_rows(n_e, tok, width):
    return -(-(CAP + n_e * tok // width) // SLOTS) * SLOTS


def each(count, step):
    if count <= 8:
        for i in range(count):
            step(i)
    else:
        lax.fori_loop(0, count, lambda i, carry: (step(i), carry)[1], 0)


def kernel(
    n_e, n_dp, units, plan,
    routes_ref, gates_ref, latent_ref, up_hbm, win_hbm, wout_hbm, cot_hbm,
    mixed, grad,
    win, wout, cot, up, dsend, drecv, act, rsend, gbuf, weight, comb, gsend, rsbuf, asend,
    load_sem, d_send, d_recv, g_send, g_recv, f_send, r_send, r_recv, a_send, a_recv,
):
    me = lax.axis_index("expert")
    dp = lax.axis_index("dp")
    n_z = n_e // CORES
    z, core = me // CORES, lax.rem(me, CORES)
    sibling = z * CORES + (CORES - 1 - core)
    if n_z == 4:
        others = [z + 1 - 2 * lax.rem(z, 2), lax.rem(z + 2, n_z), n_z - 1 - z]
    else:
        others = [lax.rem(z + off, n_z) for off in range(1, n_z)]
    z_peers = [other * CORES + core for other in others]
    f_peers = [other * CORES + (CORES - 1 - core) for other in others]
    e_peers = [lax.rem(me + off, n_e) for off in range(1, n_e)]
    dp_peers = [lax.rem(dp + off, n_dp) for off in range(1, n_dp)]

    barrier = pltpu.get_barrier_semaphore()
    for peer in e_peers:
        pl.semaphore_signal(barrier, inc=1, device_id={"expert": peer}, device_id_type=MESH)
    for peer in dp_peers:
        pl.semaphore_signal(barrier, inc=1, device_id={"dp": peer}, device_id_type=MESH)

    loads = [
        pltpu.make_async_copy(src, dst, load_sem.at[i])
        for i, (src, dst) in enumerate(
            ((win_hbm.at[0], win), (wout_hbm.at[0], wout), (cot_hbm, cot), (up_hbm, up))
        )
    ]
    for load in loads:
        load.start()

    tok = latent_ref.shape[0]
    width = latent_ref.shape[1]
    hidden = wout.shape[0]
    top = routes_ref.shape[0]
    rows = n_e * SLOTS
    cols = width // units
    chunks = len(plan)
    tall = dsend.shape[1]
    per_row = width // tok

    expert_of = lax.broadcasted_iota(jnp.int32, (n_e, tok), 0)
    named = jnp.zeros((n_e, tok), jnp.float32)
    gate = jnp.zeros((n_e, tok), jnp.float32)
    for k in range(top):
        hit = routes_ref[k : k + 1, :] == expert_of
        named = jnp.where(hit, 1.0, named)
        gate = jnp.where(hit, gates_ref[k : k + 1, :].astype(jnp.float32), gate)
    earlier = lax.broadcasted_iota(jnp.int32, (tok, tok), 0) < lax.broadcasted_iota(
        jnp.int32, (tok, tok), 1
    )
    ahead = jnp.where(earlier, 1.0, 0.0).astype(jnp.bfloat16)
    before = jnp.dot(named.astype(jnp.bfloat16), ahead, preferred_element_type=jnp.float32)
    slot = jnp.where(named > 0.0, before, -1.0)
    slot_of = lax.broadcasted_iota(jnp.int32, (SLOTS, tok), 0).astype(jnp.float32)
    pick = jnp.concatenate(
        [jnp.where(slot[e : e + 1, :] == slot_of, 1.0, 0.0) for e in range(n_e)], axis=0
    ).astype(jnp.bfloat16)
    outgoing = jnp.dot(pick, latent_ref[...], preferred_element_type=jnp.float32)
    outgoing = outgoing.reshape(n_e, SLOTS, width)
    if tall > SLOTS:
        outgoing = jnp.concatenate(
            [outgoing, jnp.zeros((n_e, tall - SLOTS, width), jnp.float32)], axis=1
        )
    row_of = lax.broadcasted_iota(jnp.int32, (tall, width), 0)
    extra = jnp.zeros((tall, width), jnp.float32)
    for i in range(n_e // per_row):
        line = jnp.concatenate(
            [gate[e : e + 1, :] for e in range(i * per_row, (i + 1) * per_row)], axis=1
        )
        extra = jnp.where(row_of == CAP + i, line, extra)
    dsend[...] = (outgoing + extra[None]).astype(jnp.bfloat16)
    drecv[me] = dsend[me]

    pl.semaphore_wait(barrier, n_e - 1 + n_dp - 1)

    def dispatch(slot_, peer):
        return pltpu.make_async_remote_copy(
            src_ref=dsend.at[peer], dst_ref=drecv.at[slot_],
            send_sem=d_send.at[peer], recv_sem=d_recv.at[slot_],
            device_id={"expert": peer}, device_id_type=MESH,
        )

    for peer in e_peers:
        dispatch(me, peer).start()
    loads[0].wait()
    for peer in e_peers:
        dispatch(peer, peer).wait_recv()

    arrived = drecv[:, :SLOTS, :].reshape(rows, width)
    tile = min(512, hidden)
    for j in range(hidden // tile):
        g = jnp.dot(arrived, win[:, j * tile : (j + 1) * tile], preferred_element_type=jnp.float32)
        u = jnp.dot(
            arrived, win[:, hidden + j * tile : hidden + (j + 1) * tile],
            preferred_element_type=jnp.float32,
        )
        act[:, j * tile : (j + 1) * tile] = (g / (1.0 + jnp.exp(-g)) * u).astype(jnp.bfloat16)

    def held(c, source):
        return gbuf.at[pl.ds(*plan[c]), source]

    def gather(c, source, peer, peer_slot, src, sems):
        return pltpu.make_async_remote_copy(
            src_ref=src, dst_ref=held(c, source),
            send_sem=sems.at[c, peer_slot], recv_sem=g_recv.at[c, source],
            device_id={"expert": peer}, device_id_type=MESH,
        )

    loads[1].wait()
    sends = []
    for c, (start, count) in enumerate(plan):
        result = jnp.dot(
            act[...], wout[:, start * cols : (start + count) * cols],
            preferred_element_type=jnp.float32,
        ).astype(jnp.bfloat16)
        for u in range(count):
            rsend[start + u] = result[:, u * cols : (u + 1) * cols]
        for i, peer in enumerate(z_peers[::-1] + [sibling]):
            copy = gather(c, me, peer, i, rsend.at[pl.ds(start, count)], g_send)
            copy.start()
            sends.append(copy)
        for u in range(count):
            gbuf[start + u, me] = result[:, u * cols : (u + 1) * cols]

    def weigh(b):
        sent = drecv[b].astype(jnp.float32)
        theirs = jnp.concatenate(
            [
                sent[CAP + e // per_row : CAP + e // per_row + 1, e % per_row * tok : (e % per_row + 1) * tok]
                for e in range(n_e)
            ],
            axis=0,
        )
        live = theirs > 0.0
        count = jnp.dot(
            jnp.where(live, 1.0, 0.0).astype(jnp.bfloat16), ahead, preferred_element_type=jnp.float32
        )
        place = jnp.where(live, count, -1.0)
        spread = jnp.concatenate(
            [
                jnp.where(place[e : e + 1, :] == slot_of, theirs[e : e + 1, :], 0.0)
                for e in range(n_e)
            ],
            axis=0,
        )
        weight[b] = spread.T.astype(jnp.bfloat16)

    each(n_e, weigh)
    loads[2].wait()

    def rows_of(c, owner):
        start, count = plan[c]
        share = count * cols // n_dp
        return pl.ds(start * cols + owner * share, share)

    def sum_rows(c):
        start, count = plan[c]
        return pl.ds(start * cols // n_dp, count * cols // n_dp)

    def scatter(c, slot_, peer):
        return pltpu.make_async_remote_copy(
            src_ref=gsend.at[rows_of(c, peer)], dst_ref=rsbuf.at[rows_of(c, slot_)],
            send_sem=r_send.at[c, peer], recv_sem=r_recv.at[c, slot_],
            device_id={"dp": peer}, device_id_type=MESH,
        )

    def spread_sum(c, slot_, peer):
        return pltpu.make_async_remote_copy(
            src_ref=asend.at[sum_rows(c)], dst_ref=grad.at[rows_of(c, slot_)],
            send_sem=a_send.at[c, peer], recv_sem=a_recv.at[c, slot_],
            device_id={"dp": peer}, device_id_type=MESH,
        )

    def reduce(c):
        total = gsend[rows_of(c, dp), :].astype(jnp.float32)
        for peer in dp_peers:
            scatter(c, peer, peer).wait_recv()
            total = total + rsbuf[rows_of(c, peer), :].astype(jnp.float32)
        total = total.astype(jnp.bfloat16)
        asend[sum_rows(c), :] = total
        for peer in dp_peers:
            spread_sum(c, dp, peer).start()
        grad[rows_of(c, dp), :] = total

    for c, (start, count) in enumerate(plan):
        left, right = start * cols, (start + count) * cols
        for i, peer in enumerate(z_peers):
            gather(c, peer, peer, i, held(c, peer), g_send).wait_recv()
            forward = gather(c, peer, sibling, i, held(c, peer), f_send)
            forward.start()
            sends.append(forward)
        gather(c, sibling, sibling, n_z - 1, held(c, sibling), g_send).wait_recv()
        for i, peer in enumerate(f_peers):
            gather(c, peer, sibling, i, held(c, peer), f_send).wait_recv()

        def combine(b):
            at = b * SLOTS
            found = jnp.concatenate(
                [
                    gbuf[u, :, pl.ds(at, SLOTS), :].reshape(rows, cols)
                    for u in range(start, start + count)
                ],
                axis=1,
            )
            comb[pl.ds(b * tok, tok), left:right] = jnp.dot(
                weight[b], found, preferred_element_type=jnp.float32
            ).astype(jnp.bfloat16)

        each(n_e, combine)
        partial = lax.dot_general(
            comb[:, left:right], cot[...], (((0,), (0,)), ((), ())),
            preferred_element_type=jnp.float32,
        )
        gsend[left:right, :] = partial.astype(jnp.bfloat16)
        for peer in dp_peers:
            scatter(c, dp, peer).start()
        if c > 0:
            reduce(c - 1)

    loads[3].wait()

    def project(b):
        at = pl.ds(b * tok, tok)
        mixed[at, :] = jnp.dot(
            comb[at, :], up[...], preferred_element_type=jnp.float32
        ).astype(jnp.bfloat16)

    half = n_e // 2
    each(half, project)
    reduce(chunks - 1)
    each(n_e - half, lambda b: project(half + b))

    for peer in e_peers:
        dispatch(me, peer).wait_send()
    for copy in sends:
        copy.wait_send()
    for c in range(chunks):
        for peer in dp_peers:
            scatter(c, dp, peer).wait_send()
            spread_sum(c, dp, peer).wait_send()
            spread_sum(c, peer, peer).wait_recv()


def finish_kernel(mixed_ref, grad_ref, mixed_out, grad_out, wide, mixed_sem, grad_sem):
    copy = pltpu.make_async_copy(mixed_ref, mixed_out, mixed_sem)
    copy.start()
    parts, deep = wide.shape[:2]
    outs = []
    for i in range(parts):
        at = pl.ds(i * deep, deep)
        wide[i] = grad_ref[at, :].astype(jnp.float32)
        outs.append(pltpu.make_async_copy(wide.at[i], grad_out.at[at], grad_sem.at[i]))
        outs[-1].start()
    copy.wait()
    for out in outs:
        out.wait()


def finish(mixed, grad):
    parts, (width, features) = 4, grad.shape
    vmem = pl.BlockSpec(memory_space=pltpu.VMEM)
    hbm = pl.BlockSpec(memory_space=pl.ANY)
    dma = pltpu.SemaphoreType.DMA
    return pl.pallas_call(
        finish_kernel,
        out_shape=(
            jax.ShapeDtypeStruct(mixed.shape, mixed.dtype),
            jax.ShapeDtypeStruct(grad.shape, jnp.float32),
        ),
        in_specs=[vmem, vmem],
        out_specs=(hbm, hbm),
        scratch_shapes=[
            pltpu.VMEM((parts, width // parts, features), jnp.float32),
            dma,
            dma((parts,)),
        ],
        compiler_params=pltpu.CompilerParams(vmem_limit_bytes=50 * 1024 * 1024),
    )(mixed, grad)


def body(n_e, n_dp, latent, up_proj, expert_in, expert_out, routes, gates, cotangent):
    tok, width = latent.shape
    hidden = expert_out.shape[1]
    group, features = cotangent.shape
    units = max(1, min(4, width // (16 * n_dp)))
    cols = width // units
    plan = [(0, 1), (1, 2), (3, 1)] if units == 4 else [(u, 1) for u in range(units)]
    chunks = len(plan)
    rows = n_e * SLOTS
    n_z = n_e // CORES
    tall = message_rows(n_e, tok, width)
    vmem = pl.BlockSpec(memory_space=pltpu.VMEM)
    hbm = pl.BlockSpec(memory_space=pl.ANY)
    bf16 = jnp.bfloat16
    dma = pltpu.SemaphoreType.DMA
    mixed, grad = pl.pallas_call(
        functools.partial(kernel, n_e, n_dp, units, plan),
        out_shape=(
            pltpu.VMEM((group, features), bf16),
            pltpu.VMEM((width, features), bf16),
        ),
        in_specs=[vmem, vmem, vmem, hbm, hbm, hbm, hbm],
        out_specs=(vmem, vmem),
        scratch_shapes=[
            pltpu.VMEM((width, 2 * hidden), bf16),
            pltpu.VMEM((hidden, width), bf16),
            pltpu.VMEM((group, features), bf16),
            pltpu.VMEM((width, features), bf16),
            pltpu.VMEM((n_e, tall, width), bf16),
            pltpu.VMEM((n_e, tall, width), bf16),
            pltpu.VMEM((rows, hidden), bf16),
            pltpu.VMEM((units, rows, cols), bf16),
            pltpu.VMEM((units, n_e, rows, cols), bf16),
            pltpu.VMEM((n_e, tok, rows), bf16),
            pltpu.VMEM((group, width), bf16),
            pltpu.VMEM((width, features), bf16),
            pltpu.VMEM((width, features), bf16),
            pltpu.VMEM((width // n_dp, features), bf16),
            dma((4,)),
            dma((n_e,)),
            dma((n_e,)),
            dma((chunks, n_z)),
            dma((chunks, n_e)),
            dma((chunks, n_z)),
            dma((chunks, n_dp)),
            dma((chunks, n_dp)),
            dma((chunks, n_dp)),
            dma((chunks, n_dp)),
        ],
        compiler_params=pltpu.CompilerParams(
            collective_id=0, has_side_effects=True, vmem_limit_bytes=54 * 1024 * 1024
        ),
        cost_estimate=pl.CostEstimate(
            flops=2 * rows * width * hidden * 3 + 4 * group * width * features,
            bytes_accessed=6 * hidden * width + 8 * group * features,
            transcendentals=rows * hidden,
        ),
    )(routes.T, gates.T, latent, up_proj, expert_in, expert_out, cotangent)
    return finish(mixed, grad)


def solution(mesh):
    in_specs = (
        P(("dp", "expert"), None),
        P(None, "expert"),
        P("expert", None, None),
        P("expert", None, None),
        P(("dp", "expert"), None),
        P(("dp", "expert"), None),
        P("dp", "expert"),
    )
    out_specs = (P("dp", "expert"), P(None, "expert"))
    return jax.shard_map(
        functools.partial(body, mesh.shape["expert"], mesh.shape["dp"]),
        mesh=mesh, in_specs=in_specs, out_specs=out_specs, check_vma=False,
    )
```

```python
import functools

import jax
import jax.numpy as jnp
from jax import lax
from jax.experimental import pallas as pl
from jax.experimental.pallas import tpu as pltpu
from jax.sharding import PartitionSpec as P

MESH = pl.DeviceIdType.MESH
SLOTS = 16
CAP = 13
CORES = 2


def message_rows(n_e, tok, width):
    return -(-(CAP + n_e * tok // width) // SLOTS) * SLOTS


def each(count, step):
    if count <= 8:
        for i in range(count):
            step(i)
    else:
        lax.fori_loop(0, count, lambda i, carry: (step(i), carry)[1], 0)


def kernel(
    n_e, n_dp, chunks,
    routes_ref, gates_ref, latent_ref, up_hbm, win_hbm, wout_hbm, cot_hbm,
    mixed, grad,
    win, wout, cot, up, dsend, drecv, act, rsend, gbuf, weight, comb, gsend, rsbuf, asend,
    load_sem, d_send, d_recv, g_send, g_recv, f_send, r_send, r_recv, a_send, a_recv,
):
    me = lax.axis_index("expert")
    dp = lax.axis_index("dp")
    n_z = n_e // CORES
    z, core = me // CORES, lax.rem(me, CORES)
    sibling = z * CORES + (CORES - 1 - core)
    z_peers = [lax.rem(z + off, n_z) * CORES + core for off in range(1, n_z)]
    f_peers = [lax.rem(z + off, n_z) * CORES + (CORES - 1 - core) for off in range(1, n_z)]
    e_peers = [lax.rem(me + off, n_e) for off in range(1, n_e)]
    dp_peers = [lax.rem(dp + off, n_dp) for off in range(1, n_dp)]

    barrier = pltpu.get_barrier_semaphore()
    for peer in e_peers:
        pl.semaphore_signal(barrier, inc=1, device_id={"expert": peer}, device_id_type=MESH)
    for peer in dp_peers:
        pl.semaphore_signal(barrier, inc=1, device_id={"dp": peer}, device_id_type=MESH)

    loads = [
        pltpu.make_async_copy(src, dst, load_sem.at[i])
        for i, (src, dst) in enumerate(
            ((win_hbm.at[0], win), (wout_hbm.at[0], wout), (cot_hbm, cot), (up_hbm, up))
        )
    ]
    for load in loads:
        load.start()

    tok = latent_ref.shape[0]
    width = latent_ref.shape[1]
    hidden = wout.shape[0]
    top = routes_ref.shape[0]
    rows = n_e * SLOTS
    cols = width // chunks
    share = cols // n_dp
    tall = dsend.shape[1]
    per_row = width // tok

    expert_of = lax.broadcasted_iota(jnp.int32, (n_e, tok), 0)
    named = jnp.zeros((n_e, tok), jnp.float32)
    gate = jnp.zeros((n_e, tok), jnp.float32)
    for k in range(top):
        hit = routes_ref[k : k + 1, :] == expert_of
        named = jnp.where(hit, 1.0, named)
        gate = jnp.where(hit, gates_ref[k : k + 1, :].astype(jnp.float32), gate)
    earlier = lax.broadcasted_iota(jnp.int32, (tok, tok), 0) < lax.broadcasted_iota(
        jnp.int32, (tok, tok), 1
    )
    ahead = jnp.where(earlier, 1.0, 0.0).astype(jnp.bfloat16)
    before = jnp.dot(named.astype(jnp.bfloat16), ahead, preferred_element_type=jnp.float32)
    slot = jnp.where(named > 0.0, before, -1.0)
    slot_of = lax.broadcasted_iota(jnp.int32, (SLOTS, tok), 0).astype(jnp.float32)
    pick = jnp.concatenate(
        [jnp.where(slot[e : e + 1, :] == slot_of, 1.0, 0.0) for e in range(n_e)], axis=0
    ).astype(jnp.bfloat16)
    outgoing = jnp.dot(pick, latent_ref[...], preferred_element_type=jnp.float32)
    outgoing = outgoing.reshape(n_e, SLOTS, width)
    if tall > SLOTS:
        outgoing = jnp.concatenate(
            [outgoing, jnp.zeros((n_e, tall - SLOTS, width), jnp.float32)], axis=1
        )
    row_of = lax.broadcasted_iota(jnp.int32, (tall, width), 0)
    extra = jnp.zeros((tall, width), jnp.float32)
    for i in range(n_e // per_row):
        line = jnp.concatenate(
            [gate[e : e + 1, :] for e in range(i * per_row, (i + 1) * per_row)], axis=1
        )
        extra = jnp.where(row_of == CAP + i, line, extra)
    dsend[...] = (outgoing + extra[None]).astype(jnp.bfloat16)
    drecv[me] = dsend[me]

    pl.semaphore_wait(barrier, n_e - 1 + n_dp - 1)

    def dispatch(slot_, peer):
        return pltpu.make_async_remote_copy(
            src_ref=dsend.at[peer], dst_ref=drecv.at[slot_],
            send_sem=d_send.at[peer], recv_sem=d_recv.at[slot_],
            device_id={"expert": peer}, device_id_type=MESH,
        )

    for peer in e_peers:
        dispatch(me, peer).start()
    loads[0].wait()
    for peer in e_peers:
        dispatch(peer, peer).wait_recv()

    arrived = drecv[:, :SLOTS, :].reshape(rows, width)
    tile = min(512, hidden)
    for j in range(hidden // tile):
        g = jnp.dot(arrived, win[:, j * tile : (j + 1) * tile], preferred_element_type=jnp.float32)
        u = jnp.dot(
            arrived, win[:, hidden + j * tile : hidden + (j + 1) * tile],
            preferred_element_type=jnp.float32,
        )
        act[:, j * tile : (j + 1) * tile] = (g / (1.0 + jnp.exp(-g)) * u).astype(jnp.bfloat16)

    def gather(c, source, peer, peer_slot, src, sems):
        return pltpu.make_async_remote_copy(
            src_ref=src, dst_ref=gbuf.at[c, source],
            send_sem=sems.at[c, peer_slot], recv_sem=g_recv.at[c, source],
            device_id={"expert": peer}, device_id_type=MESH,
        )

    loads[1].wait()
    sends = []
    for c in range(chunks):
        result = jnp.dot(
            act[...], wout[:, c * cols : (c + 1) * cols], preferred_element_type=jnp.float32
        ).astype(jnp.bfloat16)
        rsend[c] = result
        for i, peer in enumerate(z_peers + [sibling]):
            copy = gather(c, me, peer, i, rsend.at[c], g_send)
            copy.start()
            sends.append(copy)
        gbuf[c, me] = result

    def weigh(b):
        sent = drecv[b].astype(jnp.float32)
        theirs = jnp.concatenate(
            [
                sent[CAP + e // per_row : CAP + e // per_row + 1, e % per_row * tok : (e % per_row + 1) * tok]
                for e in range(n_e)
            ],
            axis=0,
        )
        live = theirs > 0.0
        count = jnp.dot(
            jnp.where(live, 1.0, 0.0).astype(jnp.bfloat16), ahead, preferred_element_type=jnp.float32
        )
        place = jnp.where(live, count, -1.0)
        spread = jnp.concatenate(
            [
                jnp.where(place[e : e + 1, :] == slot_of, theirs[e : e + 1, :], 0.0)
                for e in range(n_e)
            ],
            axis=0,
        )
        weight[b] = spread.T.astype(jnp.bfloat16)

    each(n_e, weigh)
    loads[2].wait()

    features = cot.shape[1]
    splits = [2 if c == chunks - 1 and features % 256 == 0 else 1 for c in range(chunks)]

    def lanes(c, p):
        return pl.ds(p * (features // splits[c]), features // splits[c])

    def scatter(c, p, slot_, peer):
        return pltpu.make_async_remote_copy(
            src_ref=gsend.at[c, peer, :, lanes(c, p)], dst_ref=rsbuf.at[c, slot_, :, lanes(c, p)],
            send_sem=r_send.at[c + p, peer], recv_sem=r_recv.at[c + p, slot_],
            device_id={"dp": peer}, device_id_type=MESH,
        )

    def spread_sum(c, p, slot_, peer):
        return pltpu.make_async_remote_copy(
            src_ref=asend.at[c, :, lanes(c, p)], dst_ref=grad.at[c, slot_, :, lanes(c, p)],
            send_sem=a_send.at[c + p, peer], recv_sem=a_recv.at[c + p, slot_],
            device_id={"dp": peer}, device_id_type=MESH,
        )

    def reduce(c):
        for p in range(splits[c]):
            at = lanes(c, p)
            total = gsend[c, dp, :, at].astype(jnp.float32)
            for peer in dp_peers:
                scatter(c, p, peer, peer).wait_recv()
                total = total + rsbuf[c, peer, :, at].astype(jnp.float32)
            total = total.astype(jnp.bfloat16)
            asend[c, :, at] = total
            for peer in dp_peers:
                spread_sum(c, p, dp, peer).start()
            grad[c, dp, :, at] = total

    for c in range(chunks):
        for i, peer in enumerate(z_peers):
            gather(c, peer, peer, i, rsend.at[c], g_send).wait_recv()
            forward = gather(c, peer, sibling, i, gbuf.at[c, peer], f_send)
            forward.start()
            sends.append(forward)
        gather(c, sibling, sibling, n_z - 1, rsend.at[c], g_send).wait_recv()
        for i, peer in enumerate(f_peers):
            gather(c, peer, sibling, i, rsend.at[c], f_send).wait_recv()

        def combine(b):
            at = b * SLOTS
            found = gbuf[c, :, pl.ds(at, SLOTS), :].reshape(rows, cols)
            comb[pl.ds(b * tok, tok), c * cols : (c + 1) * cols] = jnp.dot(
                weight[b], found, preferred_element_type=jnp.float32
            ).astype(jnp.bfloat16)

        each(n_e, combine)
        for p in range(splits[c]):
            at = lanes(c, p)
            partial = lax.dot_general(
                comb[:, c * cols : (c + 1) * cols], cot[:, at], (((0,), (0,)), ((), ())),
                preferred_element_type=jnp.float32,
            )
            gsend[c, :, :, at] = partial.astype(jnp.bfloat16).reshape(
                n_dp, share, features // splits[c]
            )
            for peer in dp_peers:
                scatter(c, p, dp, peer).start()
        if c > 0:
            reduce(c - 1)

    loads[3].wait()

    def project(b):
        at = pl.ds(b * tok, tok)
        mixed[at, :] = jnp.dot(
            comb[at, :], up[...], preferred_element_type=jnp.float32
        ).astype(jnp.bfloat16)

    half = n_e // 2
    each(half, project)
    reduce(chunks - 1)
    each(n_e - half, lambda b: project(half + b))

    for peer in e_peers:
        dispatch(me, peer).wait_send()
    for copy in sends:
        copy.wait_send()
    for c in range(chunks):
        for p in range(splits[c]):
            for peer in dp_peers:
                scatter(c, p, dp, peer).wait_send()
                spread_sum(c, p, dp, peer).wait_send()
                spread_sum(c, p, peer, peer).wait_recv()


def finish_kernel(mixed_ref, grad_ref, mixed_out, grad_out, wide, mixed_sem, grad_sem):
    copy = pltpu.make_async_copy(mixed_ref, mixed_out, mixed_sem)
    copy.start()
    chunks, n_dp, share = grad_ref.shape[:3]
    outs = []
    for c in range(chunks):
        wide[c] = grad_ref[c].astype(jnp.float32).reshape(n_dp * share, grad_ref.shape[3])
        at = pl.ds(c * n_dp * share, n_dp * share)
        outs.append(pltpu.make_async_copy(wide.at[c], grad_out.at[at], grad_sem.at[c]))
        outs[-1].start()
    copy.wait()
    for out in outs:
        out.wait()


def finish(mixed, grad):
    chunks, n_dp, share, features = grad.shape
    vmem = pl.BlockSpec(memory_space=pltpu.VMEM)
    hbm = pl.BlockSpec(memory_space=pl.ANY)
    dma = pltpu.SemaphoreType.DMA
    return pl.pallas_call(
        finish_kernel,
        out_shape=(
            jax.ShapeDtypeStruct(mixed.shape, mixed.dtype),
            jax.ShapeDtypeStruct((chunks * n_dp * share, features), jnp.float32),
        ),
        in_specs=[vmem, vmem],
        out_specs=(hbm, hbm),
        scratch_shapes=[
            pltpu.VMEM((chunks, n_dp * share, features), jnp.float32),
            dma,
            dma((chunks,)),
        ],
        compiler_params=pltpu.CompilerParams(vmem_limit_bytes=50 * 1024 * 1024),
    )(mixed, grad)


def body(n_e, n_dp, latent, up_proj, expert_in, expert_out, routes, gates, cotangent):
    tok, width = latent.shape
    hidden = expert_out.shape[1]
    group, features = cotangent.shape
    chunks = max(1, min(4, width // (16 * n_dp)))
    cols = width // chunks
    share = cols // n_dp
    rows = n_e * SLOTS
    n_z = n_e // CORES
    tall = message_rows(n_e, tok, width)
    vmem = pl.BlockSpec(memory_space=pltpu.VMEM)
    hbm = pl.BlockSpec(memory_space=pl.ANY)
    bf16 = jnp.bfloat16
    dma = pltpu.SemaphoreType.DMA
    mixed, grad = pl.pallas_call(
        functools.partial(kernel, n_e, n_dp, chunks),
        out_shape=(
            pltpu.VMEM((group, features), bf16),
            pltpu.VMEM((chunks, n_dp, share, features), bf16),
        ),
        in_specs=[vmem, vmem, vmem, hbm, hbm, hbm, hbm],
        out_specs=(vmem, vmem),
        scratch_shapes=[
            pltpu.VMEM((width, 2 * hidden), bf16),
            pltpu.VMEM((hidden, width), bf16),
            pltpu.VMEM((group, features), bf16),
            pltpu.VMEM((width, features), bf16),
            pltpu.VMEM((n_e, tall, width), bf16),
            pltpu.VMEM((n_e, tall, width), bf16),
            pltpu.VMEM((rows, hidden), bf16),
            pltpu.VMEM((chunks, rows, cols), bf16),
            pltpu.VMEM((chunks, n_e, rows, cols), bf16),
            pltpu.VMEM((n_e, tok, rows), bf16),
            pltpu.VMEM((group, width), bf16),
            pltpu.VMEM((chunks, n_dp, share, features), bf16),
            pltpu.VMEM((chunks, n_dp, share, features), bf16),
            pltpu.VMEM((chunks, share, features), bf16),
            dma((4,)),
            dma((n_e,)),
            dma((n_e,)),
            dma((chunks, n_z)),
            dma((chunks, n_e)),
            dma((chunks, n_z)),
            dma((chunks + 1, n_dp)),
            dma((chunks + 1, n_dp)),
            dma((chunks + 1, n_dp)),
            dma((chunks + 1, n_dp)),
        ],
        compiler_params=pltpu.CompilerParams(
            collective_id=0, has_side_effects=True, vmem_limit_bytes=54 * 1024 * 1024
        ),
        cost_estimate=pl.CostEstimate(
            flops=2 * rows * width * hidden * 3 + 4 * group * width * features,
            bytes_accessed=6 * hidden * width + 8 * group * features,
            transcendentals=rows * hidden,
        ),
    )(routes.T, gates.T, latent, up_proj, expert_in, expert_out, cotangent)
    return finish(mixed, grad)


def solution(mesh):
    in_specs = (
        P(("dp", "expert"), None),
        P(None, "expert"),
        P("expert", None, None),
        P("expert", None, None),
        P(("dp", "expert"), None),
        P(("dp", "expert"), None),
        P("dp", "expert"),
    )
    out_specs = (P("dp", "expert"), P(None, "expert"))
    return jax.shard_map(
        functools.partial(body, mesh.shape["expert"], mesh.shape["dp"]),
        mesh=mesh, in_specs=in_specs, out_specs=out_specs, check_vma=False,
    )
```
